256 devices in a mesh: row: 8 (over y, core), col: 32 (over z, x).
Axes of the slice: x: 4, y: 4, z: 8, core: 2. Of those that a mesh axis runs over, the one named last changes fastest.
Arguments:
- cotangent: bfloat16 [8192, 4096], P('col'), may hold values from -600 to 600
- token_ids: int32 [8192], replicated, may hold values from 0 to 31999, as said below
- param: float32 [32000, 4096], P('row', 'col'), may hold values from -14 to 14
- row_moment: float32 [32000], P('row'), may hold values from 1 to 120
- col_moment: float32 [4096], P('col'), may hold values from 0.1 to 1
Outputs:
- new_param: float32 [32000, 4096], P('row', 'col')
- update: float32 [32000, 4096], P('row', 'col')
- new_row: float32 [32000], P('row')
- new_col: float32 [4096], P('col')
- row_factor: float32 [32000], P('row')
The draws below stay inside these ranges and needn't reach their ends.
Inputs may be any that keep to these rules, and one draw needn't show every extreme that they name: `token_ids`: in each aligned block of 256 tokens, at most 64 ids lie in any one range of 4000 vocabulary rows starting at a multiple of 4000, and some range holds exactly 64.
All inputs are finite; a program needn't handle non-finite values.
Results may differ from the reference program's by a relative error of at most 0.0003.
Values may be sent and summed in bfloat16 or wider, within the bound.
A program may use at most 64 MiB of HBM per device.

```python
import math
import jax
import jax.numpy as jnp
from jax import lax

V = 32000
D = 4096
TOK_DEV = 256
STEP = 100
TOKENS = 8192
V_ROWS = 4000
CAP = 64
N_ROW = 8
N_COL = 32


def shuffle(single_key):
    return jax.random.permutation(single_key, TOK_DEV)


def draw_token_ids(key, part):
    key_fav, key_shift, key_perm, key_off = jax.random.split(key, 4)
    favored = jax.random.randint(key_fav, (), 0, N_ROW)
    shifts = jax.random.randint(key_shift, (N_COL, 1), 0, N_ROW - 1)
    position = jnp.arange(TOK_DEV)[None, :]
    cycled = (position - CAP) % (N_ROW - 1)
    others = (cycled + shifts) % (N_ROW - 1)
    others = others + (others >= favored).astype(jnp.int32)
    owners = jnp.where(position < CAP, favored, others)
    perms = jax.vmap(shuffle)(jax.random.split(key_perm, N_COL))
    owners = jnp.take_along_axis(owners, perms, axis=1)
    offset = jax.random.randint(key_off, (N_COL, TOK_DEV), 0, V_ROWS)
    return (owners * V_ROWS + offset).reshape(TOKENS).astype(jnp.int32)


def draw_cotangent(key, part):
    key_base, key_tok, key_col = jax.random.split(key, 3)
    tok_scale = jnp.exp(jax.random.uniform(key_tok, (TOKENS, 1), jnp.float32, 0.0, math.log(10.0)))
    column_pos = jnp.arange(D, dtype=jnp.float32)[None, :] / (D - 1)
    col_scale = jnp.exp(jax.random.uniform(key_col, (1, D), jnp.float32, 0.0, math.log(3.0))) * (1.0 + 2.0 * column_pos)
    noise = jnp.clip(jax.random.normal(key_base, (TOKENS, D), jnp.float32), -6.0, 6.0)
    return (noise * tok_scale * col_scale).astype(jnp.bfloat16)


def draw_param(key, part):
    key_base = jax.random.fold_in(key, 0)
    row_pos = jnp.arange(V, dtype=jnp.float32)[:, None] / (V - 1)
    column_pos = jnp.arange(D, dtype=jnp.float32)[None, :] / (D - 1)
    ramps = (0.5 + row_pos) * (0.5 + column_pos)
    noise = jnp.clip(jax.random.normal(key_base, (V, D), jnp.float32), -6.0, 6.0)
    return (noise * ramps).astype(jnp.float32)


def draw_row_moment(key, part):
    key = jax.random.fold_in(key, 7)
    row_pos = jnp.arange(V, dtype=jnp.float32) / (V - 1)
    spread = jnp.exp(jax.random.uniform(key, (V,), jnp.float32, 0.0, math.log(2.0)))
    values = (2.0 + 18.0 * row_pos) * spread
    return values.astype(jnp.float32)


def steps_of(rng, shape, cuts, smallest, high):
    factor_of = 1.0
    for dim, shards_of in cuts:
        heights = jax.random.uniform(jax.random.fold_in(jax.random.fold_in(rng, 6), dim), (shards_of,), jnp.float32, smallest / len(cuts), high / len(cuts))
        factor_of = factor_of * jnp.repeat(jnp.exp(heights), shape[dim] // shards_of).reshape((-1,) + (1,) * (len(shape) - 1 - dim))
    return factor_of


def setup_inputs(seed: int = 0) -> dict:
    arg_keys = jax.random.split(jax.random.key(seed), 6)
    return {
        "cotangent": draw_cotangent(jax.random.fold_in(arg_keys[5], 71), 0),
        "token_ids": draw_token_ids(jax.random.fold_in(arg_keys[5], 71), 0),
        "param": draw_param(jax.random.fold_in(arg_keys[5], 71), 0),
        "row_moment": draw_row_moment(jax.random.fold_in(arg_keys[5], 71), 0),
        "col_moment": jnp.clip(jnp.exp(math.log(1.0) - 2.3025851 * jax.random.uniform(arg_keys[4], (D,), jnp.float32) ** steps_of(arg_keys[4], (D,), ((0, 32),), -0.2, 0.2)), 0.1, 1.0),
    }


def reference(cotangent, token_ids, param, row_moment, col_moment):
    decay = 1.0 - STEP ** (-0.8)
    rate = min(0.01, STEP ** (-0.5))
    gradient = jax.ops.segment_sum(cotangent.astype(jnp.float32), token_ids, num_segments=V)
    squared = gradient * gradient + 1e-30
    new_row = decay * row_moment + (1.0 - decay) * lax.optimization_barrier(jnp.mean(squared, axis=1))
    new_col = decay * col_moment + (1.0 - decay) * lax.optimization_barrier(jnp.mean(squared, axis=0))
    row_factor = lax.rsqrt(new_row / jnp.mean(new_row))
    raw_update = gradient * row_factor[:, None] * lax.rsqrt(new_col)[None, :]
    clip_scale = jnp.maximum(1.0, jnp.sqrt(jnp.mean(raw_update * raw_update)))
    update = raw_update / clip_scale
    step_scale = rate * jnp.sqrt(jnp.mean(param * param))
    new_param = param - step_scale * update
    return (new_param, update, new_row, new_col, row_factor)
```

```python
import functools

import jax
import jax.numpy as jnp
from jax import lax
from jax.experimental import pallas as pl
from jax.experimental.pallas import tpu as pltpu
from jax.sharding import PartitionSpec as P

STEP = 100
DECAY = 1.0 - STEP ** (-0.8)
RATE = min(0.01, STEP ** (-0.5))
TINY = 1e-30
CAP = 64
BLOCK = 256
LANES = 128
NX = 4
ROW_TILE = 512
MESH = pl.DeviceIdType.MESH
F32 = jnp.float32
BF16 = jnp.bfloat16


def iota(shape, dim):
    return lax.broadcasted_iota(jnp.int32, shape, dim)


def dot(a, b):
    return jnp.dot(a, b, preferred_element_type=F32)


def dot_nt(a, b):
    return lax.dot_general(a, b, (((1,), (1,)), ((), ())), preferred_element_type=F32)


def order_of(n):
    return sorted(range(n), key=lambda d: (-min(d, n - d), d))


def step_kernel(
    n_row, n_col, local_rows, total_rows, total_cols,
    cot, ids, param, rowm, colm,
    raw_o, pv_o, r_o, nc_o, scal_o,
    cotv, posv, hiv, lov, slots, send, recv, oh, grad, sqt,
    col_recv, col_send, rs_send, rs_recv, ag_send, ag_recv, st_send, st_recv,
    cot_sem, param_sem, a2a_ssem, a2a_rsem, col_ssem, col_rsem,
    rs_ssem, rs_rsem, ag_ssem, ag_rsem, st_ssem, st_rsem,
):
    nz = n_col // NX
    rows_pad = n_col * LANES
    cells = float(total_rows) * float(total_cols)
    width = NX * LANES
    r = lax.axis_index("row")
    c = lax.axis_index("col")
    z = c // NX
    x = lax.rem(c, NX)
    order = order_of(nz)

    barrier = pltpu.get_barrier_semaphore()
    for k in range(1, n_col):
        pl.semaphore_signal(
            barrier, inc=1, device_id={"col": lax.rem(c + k, n_col)}, device_id_type=MESH
        )
    for k in range(1, n_row):
        pl.semaphore_signal(
            barrier, inc=1, device_id={"row": lax.rem(r + k, n_row)}, device_id_type=MESH
        )

    def cot_copy(j):
        zt = lax.rem(z + order[j], nz)
        return pltpu.make_async_copy(
            cot.at[:, pl.ds(pl.multiple_of(zt * width, width), width)], cotv.at[j], cot_sem.at[j]
        )

    for j in range(nz):
        cot_copy(j).start()
    param_copy = pltpu.make_async_copy(param, pv_o, param_sem)
    param_copy.start()

    local = ids[...] - r * local_rows
    inside = (local >= 0) & (local < local_rows)
    ones = jnp.where(inside, 1.0, 0.0).astype(BF16)
    before = jnp.where(iota((LANES, LANES), 0) < iota((LANES, LANES), 1), 1.0, 0.0).astype(BF16)
    count = dot(ones, before)
    total = dot(ones, jnp.ones((LANES, LANES), BF16))
    odd = lax.rem(iota(local.shape, 0), 2) == 1
    position = count + jnp.where(odd, pltpu.roll(total, 1, 0), 0.0)
    posv[...] = jnp.where(inside, position, -1000.0)
    tag = jnp.where(inside, local + 1, 0)
    hiv[...] = (tag >> 6).astype(F32)
    lov[...] = (tag & 63).astype(F32)

    slot_iota = iota((CAP, LANES), 0).astype(F32)

    def picks(row):
        return jnp.where(posv[pl.ds(row, 1), :] == slot_iota, 1.0, 0.0).astype(BF16)

    pick = jnp.concatenate([picks(2 * c), picks(2 * c + 1)], axis=1)

    def a2a_copy(j, dx):
        xt = lax.rem(x + dx, NX)
        zt = lax.rem(z + order[j], nz)
        return pltpu.make_async_remote_copy(
            src_ref=send.at[j, xt], dst_ref=recv.at[c],
            send_sem=a2a_ssem.at[j * NX + dx], recv_sem=a2a_rsem.at[c],
            device_id={"col": zt * NX + xt}, device_id_type=MESH,
        )

    def steps(j):
        return range(1, NX) if order[j] == 0 else range(NX)

    for j in range(nz):
        cot_copy(j).wait()
        packed = dot(pick, cotv[j]).astype(BF16)
        for k in range(NX):
            send[j, k] = packed[:, k * LANES:(k + 1) * LANES]
        if j == 0:
            pl.semaphore_wait(barrier, n_col + n_row - 2)
        for dx in steps(j):
            a2a_copy(j, dx).start()
        if order[j] == 0:
            recv[c] = send[j, x]

    pair_iota = iota((LANES, LANES), 0).astype(F32)
    first = iota((8, LANES), 0) == 0

    def slot_step(p, carry):
        found = jnp.zeros((8, LANES), F32)
        for h in range(4):
            row = 4 * p + h
            target = posv[pl.ds(row, 1), :] + float(CAP * (h // 2))
            onehot = jnp.where(target == pair_iota, 1.0, 0.0).astype(BF16)
            value = jnp.where(first, hiv[pl.ds(row, 1), :], lov[pl.ds(row, 1), :]).astype(BF16)
            found = found + dot_nt(value, onehot)
        slots[p] = jnp.broadcast_to(64.0 * found[0:1] + found[1:2] - 1.0, (8, LANES))
        return carry

    lax.fori_loop(0, n_col // 2, slot_step, 0)

    tile = 256
    tile_iota = iota((tile, LANES), 0).astype(F32)

    def onehot_step(i, carry):
        g = i // (rows_pad // tile)
        base = lax.rem(i, rows_pad // tile) * tile
        for h in range(2):
            wanted = slots[2 * g + h][0:1] - base.astype(F32)
            oh[g, pl.ds(pl.multiple_of(base, tile), tile), h * LANES:(h + 1) * LANES] = jnp.where(
                tile_iota == wanted, 1.0, 0.0
            ).astype(BF16)
        return carry

    lax.fori_loop(0, nz * (rows_pad // tile), onehot_step, 0)

    param_copy.wait()
    ptile = local_rows // 5

    def param_step(i, acc):
        block = pv_o[pl.ds(pl.multiple_of(i * ptile, 8), ptile), :]
        return acc + jnp.sum((block * block).reshape(ptile // 8, 8, LANES), axis=0)

    acc = lax.fori_loop(0, 5, param_step, jnp.zeros((8, LANES), F32))
    param_local = jnp.sum(jnp.sum(acc, axis=0, keepdims=True), axis=1, keepdims=True)

    mtile = min(ROW_TILE, rows_pad)
    for j in range(nz):
        zs = lax.rem(z + nz - order[j], nz)
        for dx in steps(j):
            xs = lax.rem(x + NX - dx, NX)
            src = zs * NX + xs
            pltpu.make_async_remote_copy(
                src_ref=send.at[j, 0], dst_ref=recv.at[src],
                send_sem=a2a_ssem.at[j * NX + dx], recv_sem=a2a_rsem.at[src],
                device_id={"col": src}, device_id_type=MESH,
            ).wait_recv()
        tokens = recv[pl.ds(zs * NX, NX)].reshape(NX * CAP, LANES)

        def grad_step(i, carry, j=j, zs=zs, tokens=tokens):
            rows = pl.ds(pl.multiple_of(i * mtile, mtile), mtile)
            part = dot(oh[zs, rows, :], tokens)
            grad[rows, :] = part if j == 0 else grad[rows, :] + part
            return carry

        lax.fori_loop(0, rows_pad // mtile, grad_step, 0)

    def col_step(i, acc):
        block = grad[pl.ds(pl.multiple_of(i * LANES, LANES), LANES), :]
        return acc + jnp.sum((block * block).reshape(LANES // 8, 8, LANES), axis=0)

    acc = lax.fori_loop(0, n_col, col_step, jnp.zeros((8, LANES), F32))
    col_send[0] = jnp.sum(acc, axis=0, keepdims=True)
    col_recv[r] = col_send[0]

    def over_row(src, dst, ssem, rsem):
        copies = [
            pltpu.make_async_remote_copy(
                src_ref=src.at[0], dst_ref=dst.at[r], send_sem=ssem.at[k - 1], recv_sem=rsem,
                device_id={"row": lax.rem(r + k, n_row)}, device_id_type=MESH,
            )
            for k in range(1, n_row)
        ]
        for copy in copies:
            copy.start()
        return copies

    def wait_all(buf, rsem, count):
        pltpu.make_async_copy(buf.at[pl.ds(0, count)], buf.at[pl.ds(0, count)], rsem).wait()

    col_copies = over_row(col_send, col_recv, col_ssem, col_rsem)

    def square_step(i, carry):
        block = grad[pl.ds(pl.multiple_of(i * LANES, LANES), LANES), :]
        turned = (block * block).T
        sqt[i] = turned
        rs_send[i, 0:1] = jnp.sum(turned, axis=0, keepdims=True)
        return carry

    lax.fori_loop(0, n_col, square_step, 0)

    wait_all(col_recv, col_rsem, n_row - 1)
    col_total = jnp.sum(col_recv[...], axis=0)
    new_col = DECAY * colm[...] + (1.0 - DECAY) * (col_total / float(total_rows) + TINY)
    nc_o[...] = new_col
    inverse_col = jnp.broadcast_to(1.0 / new_col, (LANES, LANES)).T

    def q_step(i, carry):
        rs_send[i, 1:2] = jnp.sum(sqt[i] * inverse_col, axis=0, keepdims=True)
        return carry

    lax.fori_loop(0, n_col, q_step, 0)

    def rs_copy(k):
        to = lax.rem(c + k, n_col)
        return pltpu.make_async_remote_copy(
            src_ref=rs_send.at[to], dst_ref=rs_recv.at[c], send_sem=rs_ssem.at[k], recv_sem=rs_rsem,
            device_id={"col": to}, device_id_type=MESH,
        )

    for k in range(1, n_col):
        rs_copy(k).start()
    rs_recv[c] = rs_send[c]
    wait_all(rs_recv, rs_rsem, n_col - 1)
    sums = jnp.sum(rs_recv[...], axis=0)

    lane = iota((1, LANES), 1)
    left = local_rows - c * LANES
    valid = lane < left
    new_row = DECAY * rowm[pl.ds(c, 1), :] + (1.0 - DECAY) * (sums[0:1] / float(total_cols) + TINY)
    row_sum = jnp.sum(jnp.where(valid, new_row, 0.0), axis=1, keepdims=True)
    raw_sum = jnp.sum(jnp.where(valid, sums[1:2] / new_row, 0.0), axis=1, keepdims=True)
    stats = jnp.where(lane == 0, row_sum, jnp.where(lane == 1, raw_sum, jnp.where(lane == 2, param_local, 0.0)))
    ag_send[0] = jnp.concatenate([new_row, stats], axis=0)
    ag_recv[c] = ag_send[0]

    def ag_copy(k):
        return pltpu.make_async_remote_copy(
            src_ref=ag_send.at[0], dst_ref=ag_recv.at[c], send_sem=ag_ssem.at[k], recv_sem=ag_rsem,
            device_id={"col": lax.rem(c + k, n_col)}, device_id_type=MESH,
        )

    for k in range(1, n_col):
        ag_copy(k).start()
    wait_all(ag_recv, ag_rsem, n_col - 1)
    gathered = ag_recv[...]
    st_send[0] = jnp.sum(gathered, axis=0)[1:2]
    st_recv[r] = st_send[0]
    st_copies = over_row(st_send, st_recv, st_ssem, st_rsem)

    rows_all = gathered[:, 0, :]
    r_o[...] = rows_all
    col_rsqrt = lax.rsqrt(new_col)
    full = local_rows // LANES
    rest = local_rows - full * LANES

    def scaled(i, size):
        factor = jnp.broadcast_to(lax.rsqrt(ag_recv[i][0:1]), (LANES, LANES)).T
        block = grad[pl.ds(pl.multiple_of(i * LANES, LANES), size), :]
        return block * factor[:size] * col_rsqrt

    def raw_step(i, carry):
        raw_o[pl.ds(pl.multiple_of(i * LANES, LANES), LANES), :] = scaled(i, LANES)
        return carry

    lax.fori_loop(0, full, raw_step, 0)
    if rest:
        raw_o[full * LANES:local_rows, :] = scaled(full, rest)

    wait_all(st_recv, st_rsem, n_row - 1)
    totals = jnp.sum(st_recv[...], axis=0)

    def pick_lane(k):
        return jnp.broadcast_to(
            jnp.sum(jnp.where(lane == k, totals, 0.0), axis=1, keepdims=True), (1, LANES)
        )

    mean_row = pick_lane(0) / float(total_rows)
    clip = jnp.maximum(1.0, jnp.sqrt(mean_row * pick_lane(1) / cells))
    root = jnp.sqrt(mean_row)
    step = RATE * jnp.sqrt(pick_lane(2) / cells)
    scal_o[0:1, :] = root / clip
    scal_o[1:2, :] = step
    scal_o[2:3, :] = root
    scal_o[3:8, :] = jnp.zeros((5, LANES), F32)

    for j in range(nz):
        for dx in steps(j):
            a2a_copy(j, dx).wait_send()
    for copy in col_copies + st_copies:
        copy.wait_send()
    for k in range(1, n_col):
        rs_copy(k).wait_send()
        ag_copy(k).wait_send()


def write_kernel(
    local_rows, raw, pv, rows, new_col, scal,
    np_o, up_o, nr_o, nc_o, rf_o,
    npv, upv, nrv, ncv, rfv, out_sem, small_sem,
):
    count = 10
    size = local_rows // count
    k = scal[0:1, :]
    step = scal[1:2, :]
    root = scal[2:3, :]
    copies = []
    for i in range(count):
        span = pl.ds(i * size, size)
        update = raw[span, :] * k
        upv[span, :] = update
        copies.append(pltpu.make_async_copy(upv.at[span], up_o.at[span], out_sem.at[0, i]))
        copies[-1].start()
        npv[span, :] = pv[span, :] - step * update
        copies.append(pltpu.make_async_copy(npv.at[span], np_o.at[span], out_sem.at[1, i]))
        copies[-1].start()
        if i == 0:
            values = rows[...]
            factor = lax.rsqrt(values) * root
            for j in range(pl.cdiv(local_rows, LANES)):
                n = min(LANES, local_rows - j * LANES)
                nrv[pl.ds(j * LANES, n)] = values[j, :n]
                rfv[pl.ds(j * LANES, n)] = factor[j, :n]
            ncv[...] = new_col[0, :]
            for q, (src, dst) in enumerate(((nrv, nr_o), (rfv, rf_o), (ncv, nc_o))):
                copies.append(pltpu.make_async_copy(src, dst, small_sem.at[q]))
                copies[-1].start()
    for copy in copies:
        copy.wait()


def body(n_row, n_col, cotangent, token_ids, param, row_moment, col_moment):
    local_rows, width = param.shape
    total_rows = local_rows * n_row
    total_cols = width * n_col
    rows_pad = n_col * LANES
    nz = n_col // NX
    vmem = pl.BlockSpec(memory_space=pltpu.VMEM)
    hbm = pl.BlockSpec(memory_space=pltpu.HBM)
    dma = pltpu.SemaphoreType.DMA

    ids = token_ids.reshape(n_col * BLOCK // LANES, LANES)
    rowm = jnp.pad(row_moment, (0, rows_pad - local_rows), constant_values=1.0).reshape(n_col, LANES)
    raw, pv, rows, new_col, scal = pl.pallas_call(
        functools.partial(step_kernel, n_row, n_col, local_rows, total_rows, total_cols),
        out_shape=(
            pltpu.VMEM((local_rows, LANES), F32),
            pltpu.VMEM((local_rows, LANES), F32),
            pltpu.VMEM((n_col, LANES), F32),
            pltpu.VMEM((1, LANES), F32),
            pltpu.VMEM((8, LANES), F32),
        ),
        in_specs=[hbm, vmem, hbm, vmem, vmem],
        out_specs=(vmem,) * 5,
        scratch_shapes=[
            pltpu.VMEM((nz, BLOCK, NX * LANES), BF16),
            pltpu.VMEM(ids.shape, F32),
            pltpu.VMEM(ids.shape, F32),
            pltpu.VMEM(ids.shape, F32),
            pltpu.VMEM((n_col // 2, 8, LANES), F32),
            pltpu.VMEM((nz, NX, CAP, LANES), BF16),
            pltpu.VMEM((n_col, CAP, LANES), BF16),
            pltpu.VMEM((nz, rows_pad, NX * CAP), BF16),
            pltpu.VMEM((rows_pad, LANES), F32),
            pltpu.VMEM((n_col, LANES, LANES), F32),
            pltpu.VMEM((n_row, 1, LANES), F32),
            pltpu.VMEM((1, 1, LANES), F32),
            pltpu.VMEM((n_col, 2, LANES), F32),
            pltpu.VMEM((n_col, 2, LANES), F32),
            pltpu.VMEM((1, 2, LANES), F32),
            pltpu.VMEM((n_col, 2, LANES), F32),
            pltpu.VMEM((1, 1, LANES), F32),
            pltpu.VMEM((n_row, 1, LANES), F32),
            dma((nz,)),
            dma,
            dma((n_col,)),
            dma((n_col,)),
            dma((n_row,)),
            dma,
            dma((n_col,)),
            dma,
            dma((n_col,)),
            dma,
            dma((n_row,)),
            dma,
        ],
        compiler_params=pltpu.CompilerParams(
            collective_id=0, has_side_effects=True, vmem_limit_bytes=44 * 1024 * 1024
        ),
        name="adafactor_step",
    )(cotangent, ids, param, rowm, col_moment.reshape(1, LANES))

    return pl.pallas_call(
        functools.partial(write_kernel, local_rows),
        out_shape=(
            jax.ShapeDtypeStruct((local_rows, LANES), F32),
            jax.ShapeDtypeStruct((local_rows, LANES), F32),
            jax.ShapeDtypeStruct((local_rows,), F32),
            jax.ShapeDtypeStruct((LANES,), F32),
            jax.ShapeDtypeStruct((local_rows,), F32),
        ),
        in_specs=[vmem] * 5,
        out_specs=(hbm,) * 5,
        scratch_shapes=[
            pltpu.VMEM((local_rows, LANES), F32),
            pltpu.VMEM((local_rows, LANES), F32),
            pltpu.VMEM((local_rows,), F32),
            pltpu.VMEM((LANES,), F32),
            pltpu.VMEM((local_rows,), F32),
            dma((2, 10)),
            dma((3,)),
        ],
        compiler_params=pltpu.CompilerParams(vmem_limit_bytes=16 * 1024 * 1024),
        name="adafactor_write",
    )(raw, pv, rows, new_col, scal)


def solution(mesh):
    n_row, n_col = mesh.shape["row"], mesh.shape["col"]
    in_specs = (P("col", None), P(), P("row", "col"), P("row"), P("col"))
    out_specs = (P("row", "col"), P("row", "col"), P("row"), P("col"), P("row"))
    return jax.shard_map(
        functools.partial(body, n_row, n_col),
        mesh=mesh, in_specs=in_specs, out_specs=out_specs, check_vma=False,
    )
```

```python
import functools

import jax
import jax.numpy as jnp
from jax import lax
from jax.experimental import pallas as pl
from jax.experimental.pallas import tpu as pltpu
from jax.sharding import PartitionSpec as P

STEP = 100
DECAY = 1.0 - STEP ** (-0.8)
RATE = min(0.01, STEP ** (-0.5))
TINY = 1e-30
CAP = 64
BLOCK = 256
LANES = 128
NX = 4
MESH = pl.DeviceIdType.MESH
F32 = jnp.float32
BF16 = jnp.bfloat16


def iota(shape, dim):
    return lax.broadcasted_iota(jnp.int32, shape, dim)


def dot(a, b):
    return jnp.dot(a, b, preferred_element_type=F32)


def dot_nt(a, b):
    return lax.dot_general(a, b, (((1,), (1,)), ((), ())), preferred_element_type=F32)


def order_of(nz):
    return sorted(range(nz), key=lambda d: (-min(d, nz - d), d))


def step_kernel(
    n_row, n_col, local_rows, total_rows, total_cols,
    cot, ids_hbm, param, rowm_hbm, colm_hbm,
    raw_o, pv_o, r_o, nc_o, scal_o,
    cotv, ids, rowm, moments, colm, posv, hiv, lov, high, low, send, recv, grad,
    col_send, col_recv, rs_send, rs_recv, zb_send, zb_recv, q_send, q_recv,
    ag_recv, sc_send, sc_recv, st_send, st_recv,
    in_sem, cot_sem, a2a_ssem, a2a_rsem, ssem, rsem,
):
    nz = n_col // NX
    cells = float(total_rows) * float(total_cols)
    width = NX * LANES
    r = lax.axis_index("row")
    c = lax.axis_index("col")
    z = c // NX
    x = lax.rem(c, NX)
    order = order_of(nz)

    barrier = pltpu.get_barrier_semaphore()
    for dz in order:
        for dx in (2, 1, 3, 0):
            if dz or dx:
                peer = lax.rem(z + dz, nz) * NX + lax.rem(x + dx, NX)
                pl.semaphore_signal(barrier, inc=1, device_id={"col": peer}, device_id_type=MESH)
    for k in range(1, n_row):
        pl.semaphore_signal(
            barrier, inc=1, device_id={"row": lax.rem(r + k, n_row)}, device_id_type=MESH
        )

    ids_copy = pltpu.make_async_copy(ids_hbm, ids, in_sem.at[0])
    ids_copy.start()

    def cot_copy(j):
        zt = lax.rem(z + order[j], nz)
        return pltpu.make_async_copy(
            cot.at[:, pl.ds(pl.multiple_of(zt * width, width), width)], cotv.at[j], cot_sem.at[j]
        )

    for j in range(nz):
        cot_copy(j).start()

    rowm_copy = pltpu.make_async_copy(rowm_hbm, rowm, in_sem.at[1])
    rowm_copy.start()
    colm_copy = pltpu.make_async_copy(colm_hbm, colm, in_sem.at[2])
    colm_copy.start()
    param_copy = pltpu.make_async_copy(param, pv_o, in_sem.at[3])
    param_copy.start()

    ids_copy.wait()
    local = ids[...] - r * local_rows
    inside = (local >= 0) & (local < local_rows)
    ones = jnp.where(inside, 1.0, 0.0).astype(BF16)
    before = jnp.where(iota((LANES, LANES), 0) < iota((LANES, LANES), 1), 1.0, 0.0).astype(BF16)
    count = dot(ones, before)
    total = dot(ones, jnp.ones((LANES, LANES), BF16))
    odd = lax.rem(iota(local.shape, 0), 2) == 1
    position = count + jnp.where(odd, pltpu.roll(total, 1, 0), 0.0)
    posv[...] = jnp.where(inside, position, -1000.0)
    hiv[...] = jnp.where(inside, (local >> 7) + 1, 0).astype(F32)
    lov[...] = jnp.where(inside, local & 127, 0).astype(F32)

    slot_iota = iota((CAP, LANES), 0).astype(F32)

    def picks(block):
        return jnp.concatenate(
            [
                jnp.where(posv[pl.ds(2 * block + h, 1), :] == slot_iota, 1.0, 0.0).astype(BF16)
                for h in range(2)
            ],
            axis=1,
        )

    pick = picks(c)

    def a2a_copy(j, dx):
        xt = lax.rem(x + dx, NX)
        zt = lax.rem(z + order[j], nz)
        return pltpu.make_async_remote_copy(
            src_ref=send.at[j, xt], dst_ref=recv.at[c],
            send_sem=a2a_ssem.at[j * NX + dx], recv_sem=a2a_rsem.at[c],
            device_id={"col": zt * NX + xt}, device_id_type=MESH,
        )

    def steps(j):
        return range(1, NX) if j == nz - 1 else range(NX)

    for j in range(nz):
        cot_copy(j).wait()
        packed = dot(pick, cotv[j]).astype(BF16)
        for k in range(NX):
            send[j, k] = packed[:, k * LANES:(k + 1) * LANES]
    recv[c] = send[nz - 1, x]
    pl.semaphore_wait(barrier, n_col + n_row - 2)
    for j in range(nz):
        for dx in steps(j):
            a2a_copy(j, dx).start()

    lane_iota = iota((CAP, LANES), 1).astype(F32)

    def slot_step(b, carry):
        g = b // NX
        span = pl.ds(pl.multiple_of(lax.rem(b, NX) * CAP, CAP), CAP)
        found = jnp.zeros((CAP, 2 * LANES), F32)
        both = picks(b)
        for h in range(2):
            row = pl.ds(2 * b + h, 1)
            values = jnp.concatenate(
                [
                    jnp.broadcast_to(hiv[row, :], (LANES, LANES)),
                    jnp.broadcast_to(lov[row, :], (LANES, LANES)),
                ],
                axis=0,
            ).astype(BF16)
            found = found + dot_nt(both[:, h * LANES:(h + 1) * LANES], values)
        high[g, span, :] = found[:, :LANES].astype(BF16)
        low[g, span, :] = jnp.where(found[:, LANES:] == lane_iota, 1.0, 0.0).astype(BF16)
        return carry

    lax.fori_loop(0, n_col, slot_step, 0, unroll=8)

    param_copy.wait()
    ptile = local_rows // 5

    def param_step(i, acc):
        block = pv_o[pl.ds(pl.multiple_of(i * ptile, 8), ptile), :]
        return acc + jnp.sum((block * block).reshape(ptile // 8, 8, LANES), axis=0)

    acc = lax.fori_loop(0, 5, param_step, jnp.zeros((8, LANES), F32))
    param_local = jnp.sum(jnp.sum(acc, axis=0, keepdims=True), axis=1, keepdims=True)

    grad[...] = jnp.zeros_like(grad)


    def wait_group(j, dxs):
        zs = lax.rem(z + nz - order[j], nz)
        for dx in dxs:
            src = zs * NX + lax.rem(x + NX - dx, NX)
            pltpu.make_async_remote_copy(
                src_ref=send.at[0, 0], dst_ref=recv.at[src],
                send_sem=a2a_ssem.at[0], recv_sem=a2a_rsem.at[src],
                device_id={"col": src}, device_id_type=MESH,
            ).wait_recv()
        return zs

    def parts(zs):
        turned = recv[pl.ds(zs * NX, NX)].reshape(NX * CAP, LANES).T
        hi, lo = high[zs], low[zs]
        zero = jnp.zeros_like(lo)
        for i in range(n_col // 2):
            onehot = jnp.concatenate(
                [jnp.where(hi == jnp.asarray(2 * i + h + 1, BF16), lo, zero) for h in range(2)], axis=1
            )
            part = dot(turned, onehot)
            for h in range(2):
                yield 2 * i + h, part[:, h * LANES:(h + 1) * LANES]

    for j in range(nz - 1):
        for i, part in parts(wait_group(j, steps(j))):
            grad[i] += part
    zs = wait_group(nz - 1, steps(nz - 1))
    acc = jnp.zeros((LANES, LANES), F32)
    for i, part in parts(zs):
        value = grad[i] + part
        grad[i] = value
        value = value * value
        acc = acc + value
        rs_send[i // nz, pl.ds(i % nz, 1), :] = jnp.sum(value, axis=0, keepdims=True)

    def exchange(src, dst, me, axis, q, count):
        copies = []
        for k in range(1, count):
            if axis == "row":
                device = {"row": lax.rem(r + k, n_row)}
                to = lax.rem(r + k, n_row)
            elif axis == "x":
                to = lax.rem(x + k, NX)
                device = {"col": z * NX + to}
            elif axis == "z":
                to = lax.rem(z + k, nz)
                device = {"col": to * NX + x}
            else:
                to = lax.rem(c + k, n_col)
                device = {"col": to}
            copies.append(
                pltpu.make_async_remote_copy(
                    src_ref=src.at[to] if src.shape[0] > 1 else src.at[0], dst_ref=dst.at[me],
                    send_sem=ssem.at[q, k], recv_sem=rsem.at[q],
                    device_id=device, device_id_type=MESH,
                )
            )
            copies[-1].start()
        return copies

    def wait_all(buf, q):
        rest = buf.at[pl.ds(0, buf.shape[0] - 1)]
        pltpu.make_async_copy(rest, rest, rsem.at[q]).wait()

    copies = exchange(rs_send, rs_recv, x, "x", 1, NX)
    col_send[0] = jnp.sum(acc.T, axis=0, keepdims=True)
    copies += exchange(col_send, col_recv, r, "row", 0, n_row)
    rs_recv[x] = rs_send[x]
    col_recv[r] = col_send[0]
    colm_copy.wait()
    rowm_copy.wait()
    for i in range(n_col):
        size = max(0, min(LANES, local_rows - i * LANES))
        if size < LANES:
            moments[pl.ds(i, 1), :] = jnp.ones((1, LANES), F32)
        if size:
            moments[i, :size] = rowm[pl.ds(i * LANES, size)]

    wait_all(rs_recv, 1)
    zb_send[0] = jnp.sum(rs_recv[...], axis=0)
    copies += exchange(zb_send, zb_recv, z, "z", 2, nz)
    zb_recv[z] = zb_send[0]

    wait_all(col_recv, 0)
    col_total = jnp.sum(col_recv[...], axis=0)
    new_col = DECAY * colm[...] + (1.0 - DECAY) * (col_total / float(total_rows) + TINY)
    nc_o[...] = new_col
    turned_col = jnp.broadcast_to(new_col, (LANES, LANES)).T
    inverse_col = 1.0 / turned_col
    for i in range(n_col):
        value = grad[i]
        q_send[i // nz, pl.ds(i % nz, 1), :] = jnp.sum(value * value * inverse_col, axis=0, keepdims=True)
    copies += exchange(q_send, q_recv, x, "x", 3, NX)
    q_recv[x] = q_send[x]

    wait_all(zb_recv, 2)
    row_total = jnp.sum(zb_recv[...], axis=0)
    moment = moments[pl.ds(pl.multiple_of(x * nz, nz), nz), :]
    new_row = DECAY * moment + (1.0 - DECAY) * (row_total / float(total_cols) + TINY)
    ag_recv[x] = new_row
    copies += exchange(ag_recv.at[pl.ds(x, 1)], ag_recv, x, "x", 4, NX)
    wait_all(q_recv, 3)
    row_id = x * (nz * LANES) + iota((nz, LANES), 0) * LANES + iota((nz, LANES), 1)
    valid = row_id < local_rows
    raw_part = jnp.sum(q_recv[...], axis=0) / new_row

    def total_of(value):
        return jnp.sum(jnp.sum(jnp.where(valid, value, 0.0), axis=0, keepdims=True), axis=1, keepdims=True)

    lane = iota((1, LANES), 1)
    row_sum = total_of(new_row) * (1.0 / nz)
    raw_sum = total_of(raw_part)
    sc_send[0] = jnp.where(
        lane == 0, row_sum, jnp.where(lane == 1, raw_sum, jnp.where(lane == 2, param_local, 0.0))
    )
    copies += exchange(sc_send, sc_recv, c, "col", 5, n_col)
    sc_recv[c] = sc_send[0]

    wait_all(ag_recv, 4)
    r_o[...] = ag_recv[...].reshape(n_col, LANES)
    col_rsqrt = lax.rsqrt(turned_col)

    def raw_chunk(i):
        size = min(LANES, local_rows - i * LANES)
        factor = lax.rsqrt(ag_recv[i // nz, pl.ds(i % nz, 1), :])
        raw_o[pl.ds(i * LANES, size), :] = (grad[i] * factor * col_rsqrt).T[:size]

    chunks = pl.cdiv(local_rows, LANES)
    for i in range(chunks // 2):
        raw_chunk(i)
    wait_all(sc_recv, 5)
    st_send[0] = jnp.sum(sc_recv[...], axis=0)
    copies += exchange(st_send, st_recv, r, "row", 6, n_row)
    st_recv[r] = st_send[0]
    for i in range(chunks // 2, chunks):
        raw_chunk(i)
    wait_all(st_recv, 6)
    totals = jnp.sum(st_recv[...], axis=0)

    def pick_lane(k):
        return jnp.broadcast_to(
            jnp.sum(jnp.where(lane == k, totals, 0.0), axis=1, keepdims=True), (1, LANES)
        )

    mean_row = pick_lane(0) / float(total_rows)
    clip = jnp.maximum(1.0, jnp.sqrt(mean_row * pick_lane(1) / cells))
    root = jnp.sqrt(mean_row)
    step = RATE * jnp.sqrt(pick_lane(2) / cells)
    scal_o[0:1, :] = root / clip
    scal_o[1:2, :] = step
    scal_o[2:3, :] = root
    scal_o[3:8, :] = jnp.zeros((5, LANES), F32)

    for j in range(nz):
        for dx in steps(j):
            a2a_copy(j, dx).wait_send()
    for copy in copies:
        copy.wait_send()


def write_kernel(
    local_rows, raw, pv, rows, new_col, scal,
    np_o, up_o, nr_o, nc_o, rf_o,
    npv, upv, nrv, ncv, rfv, out_sem, small_sem,
):
    count = 10
    size = local_rows // count
    k = scal[0:1, :]
    step = scal[1:2, :]
    root = scal[2:3, :]
    copies = []
    for i in range(count):
        span = pl.ds(i * size, size)
        update = raw[span, :] * k
        upv[span, :] = update
        copies.append(pltpu.make_async_copy(upv.at[span], up_o.at[span], out_sem.at[0, i]))
        copies[-1].start()
        npv[span, :] = pv[span, :] - step * update
        copies.append(pltpu.make_async_copy(npv.at[span], np_o.at[span], out_sem.at[1, i]))
        copies[-1].start()
        if i == 0:
            values = rows[...]
            factor = lax.rsqrt(values) * root
            for j in range(pl.cdiv(local_rows, LANES)):
                n = min(LANES, local_rows - j * LANES)
                nrv[pl.ds(j * LANES, n)] = values[j, :n]
                rfv[pl.ds(j * LANES, n)] = factor[j, :n]
            ncv[...] = new_col[0, :]
            for q, (src, dst) in enumerate(((nrv, nr_o), (rfv, rf_o), (ncv, nc_o))):
                copies.append(pltpu.make_async_copy(src, dst, small_sem.at[q]))
                copies[-1].start()
    for copy in copies:
        copy.wait()


def body(n_row, n_col, cotangent, token_ids, param, row_moment, col_moment):
    local_rows, width = param.shape
    total_rows = local_rows * n_row
    total_cols = width * n_col
    nz = n_col // NX
    vmem = pl.BlockSpec(memory_space=pltpu.VMEM)
    hbm = pl.BlockSpec(memory_space=pltpu.HBM)
    dma = pltpu.SemaphoreType.DMA

    ids_shape = (n_col * BLOCK // LANES, LANES)

    def stay(value):
        return pltpu.with_memory_space_constraint(value, pltpu.HBM)

    raw, pv, rows, new_col, scal = pl.pallas_call(
        functools.partial(step_kernel, n_row, n_col, local_rows, total_rows, total_cols),
        out_shape=(
            pltpu.VMEM((local_rows, LANES), F32),
            pltpu.VMEM((local_rows, LANES), F32),
            pltpu.VMEM((n_col, LANES), F32),
            pltpu.VMEM((1, LANES), F32),
            pltpu.VMEM((8, LANES), F32),
        ),
        in_specs=[hbm] * 5,
        out_specs=(vmem,) * 5,
        scratch_shapes=[
            pltpu.VMEM((nz, BLOCK, NX * LANES), BF16),
            pltpu.VMEM(ids_shape, jnp.int32),
            pltpu.VMEM((local_rows,), F32),
            pltpu.VMEM((n_col, LANES), F32),
            pltpu.VMEM((1, LANES), F32),
            pltpu.VMEM(ids_shape, F32),
            pltpu.VMEM(ids_shape, F32),
            pltpu.VMEM(ids_shape, F32),
            pltpu.VMEM((nz, NX * CAP, LANES), BF16),
            pltpu.VMEM((nz, NX * CAP, LANES), BF16),
            pltpu.VMEM((nz, NX, CAP, LANES), BF16),
            pltpu.VMEM((n_col, CAP, LANES), BF16),
            pltpu.VMEM((n_col, LANES, LANES), F32),
            pltpu.VMEM((1, 1, LANES), F32),
            pltpu.VMEM((n_row, 1, LANES), F32),
            pltpu.VMEM((NX, nz, LANES), F32),
            pltpu.VMEM((NX, nz, LANES), F32),
            pltpu.VMEM((1, nz, LANES), F32),
            pltpu.VMEM((nz, nz, LANES), F32),
            pltpu.VMEM((NX, nz, LANES), F32),
            pltpu.VMEM((NX, nz, LANES), F32),
            pltpu.VMEM((NX, nz, LANES), F32),
            pltpu.VMEM((1, 1, LANES), F32),
            pltpu.VMEM((n_col, 1, LANES), F32),
            pltpu.VMEM((1, 1, LANES), F32),
            pltpu.VMEM((n_row, 1, LANES), F32),
            dma((4,)),
            dma((nz,)),
            dma((n_col,)),
            dma((n_col,)),
            dma((7, max(n_col, n_row))),
            dma((7,)),
        ],
        compiler_params=pltpu.CompilerParams(
            collective_id=0, has_side_effects=True, vmem_limit_bytes=32 * 1024 * 1024
        ),
        name="adafactor_step",
    )(
        stay(cotangent), stay(token_ids.reshape(ids_shape)), stay(param), stay(row_moment),
        stay(col_moment.reshape(1, LANES)),
    )

    return pl.pallas_call(
        functools.partial(write_kernel, local_rows),
        out_shape=(
            jax.ShapeDtypeStruct((local_rows, LANES), F32),
            jax.ShapeDtypeStruct((local_rows, LANES), F32),
            jax.ShapeDtypeStruct((local_rows,), F32),
            jax.ShapeDtypeStruct((LANES,), F32),
            jax.ShapeDtypeStruct((local_rows,), F32),
        ),
        in_specs=[vmem] * 5,
        out_specs=(hbm,) * 5,
        scratch_shapes=[
            pltpu.VMEM((local_rows, LANES), F32),
            pltpu.VMEM((local_rows, LANES), F32),
            pltpu.VMEM((local_rows,), F32),
            pltpu.VMEM((LANES,), F32),
            pltpu.VMEM((local_rows,), F32),
            dma((2, 10)),
            dma((3,)),
        ],
        compiler_params=pltpu.CompilerParams(vmem_limit_bytes=16 * 1024 * 1024),
        name="adafactor_write",
    )(raw, pv, rows, new_col, scal)


def solution(mesh):
    n_row, n_col = mesh.shape["row"], mesh.shape["col"]
    in_specs = (P("col", None), P(), P("row", "col"), P("row"), P("col"))
    out_specs = (P("row", "col"), P("row", "col"), P("row"), P("col"), P("row"))
    return jax.shard_map(
        functools.partial(body, n_row, n_col),
        mesh=mesh, in_specs=in_specs, out_specs=out_specs, check_vma=False,
    )
```

```python
import functools

import jax
import jax.numpy as jnp
from jax import lax
from jax.experimental import pallas as pl
from jax.experimental.pallas import tpu as pltpu
from jax.sharding import PartitionSpec as P

STEP = 100
DECAY = 1.0 - STEP ** (-0.8)
RATE = min(0.01, STEP ** (-0.5))
TINY = 1e-30
CAP = 64
BLOCK = 256
LANES = 128
NX = 4
GROUP = 4
MESH = pl.DeviceIdType.MESH
F32 = jnp.float32
BF16 = jnp.bfloat16


def iota(shape, dim):
    return lax.broadcasted_iota(jnp.int32, shape, dim)


def dot(a, b):
    return jnp.dot(a, b, preferred_element_type=F32)


def dot_nt(a, b):
    return lax.dot_general(a, b, (((1,), (1,)), ((), ())), preferred_element_type=F32)


def order_of(nz):
    far = sorted(range(nz), key=lambda d: (-min(d, nz - d), d))
    return [(dz, dx) for dx in (2, 1, 3, 0) for dz in far]


def step_kernel(
    n_row, n_col, local_rows, total_rows, total_cols,
    cot, ids_hbm, param, rowm_hbm, colm_hbm,
    raw_o, pv_o, r_o, nc_o, scal_o,
    cotv, ids, rowm, moments, colm, posv, hiv, lov, high, low, send, recv, grad,
    col_send, col_recv, rs_send, rs_recv, q_send, q_recv,
    ag_recv, sc_send, sc_recv, st_send, st_recv,
    in_sem, cot_sem, a2a_ssem, a2a_rsem, ssem, rsem,
):
    nz = n_col // NX
    cells = float(total_rows) * float(total_cols)
    width = NX * LANES
    r = lax.axis_index("row")
    c = lax.axis_index("col")
    z = c // NX
    x = lax.rem(c, NX)
    order = order_of(nz)

    barrier = pltpu.get_barrier_semaphore()
    for dz, dx in order[:-1]:
        peer = lax.rem(z + dz, nz) * NX + lax.rem(x + dx, NX)
        pl.semaphore_signal(barrier, inc=1, device_id={"col": peer}, device_id_type=MESH)
    for k in range(1, n_row):
        pl.semaphore_signal(
            barrier, inc=1, device_id={"row": lax.rem(r + k, n_row)}, device_id_type=MESH
        )

    ids_copy = pltpu.make_async_copy(ids_hbm, ids, in_sem.at[0])
    ids_copy.start()

    def cot_copy(j):
        zt = lax.rem(z + j, nz)
        return pltpu.make_async_copy(
            cot.at[:, pl.ds(pl.multiple_of(zt * width, width), width)], cotv.at[j], cot_sem.at[j]
        )

    for j in range(nz):
        cot_copy(j).start()

    rowm_copy = pltpu.make_async_copy(rowm_hbm, rowm, in_sem.at[1])
    rowm_copy.start()
    colm_copy = pltpu.make_async_copy(colm_hbm, colm, in_sem.at[2])
    colm_copy.start()
    param_copy = pltpu.make_async_copy(param, pv_o, in_sem.at[3])
    param_copy.start()

    ids_copy.wait()
    local = ids[...] - r * local_rows
    inside = (local >= 0) & (local < local_rows)
    ones = jnp.where(inside, 1.0, 0.0).astype(BF16)
    before = jnp.where(iota((LANES, LANES), 0) < iota((LANES, LANES), 1), 1.0, 0.0).astype(BF16)
    count = dot(ones, before)
    total = dot(ones, jnp.ones((LANES, LANES), BF16))
    odd = lax.rem(iota(local.shape, 0), 2) == 1
    position = count + jnp.where(odd, pltpu.roll(total, 1, 0), 0.0)
    posv[...] = jnp.where(inside, position, -1000.0)
    hiv[...] = jnp.where(inside, (local >> 7) + 1, 0).astype(F32)
    lov[...] = jnp.where(inside, local & 127, 0).astype(F32)

    slot_iota = iota((CAP, LANES), 0).astype(F32)

    def picks(block):
        return jnp.concatenate(
            [
                jnp.where(posv[pl.ds(2 * block + h, 1), :] == slot_iota, 1.0, 0.0).astype(BF16)
                for h in range(2)
            ],
            axis=1,
        )

    pick = picks(c)

    for j in range(nz):
        cot_copy(j).wait()
        packed = dot(pick, cotv[j]).astype(BF16)
        for k in range(NX):
            send[j, k] = packed[:, k * LANES:(k + 1) * LANES]
    recv[c] = send[0, x]
    pl.semaphore_wait(barrier, n_col + n_row - 2)
    for n, (dz, dx) in enumerate(order[:-1]):
        xt = lax.rem(x + dx, NX)
        pltpu.make_async_remote_copy(
            src_ref=send.at[dz, xt], dst_ref=recv.at[c],
            send_sem=a2a_ssem, recv_sem=a2a_rsem.at[n // GROUP],
            device_id={"col": lax.rem(z + dz, nz) * NX + xt}, device_id_type=MESH,
        ).start()

    lane_iota = iota((CAP, LANES), 1).astype(F32)

    def slot_step(b, carry):
        found = jnp.zeros((CAP, 2 * LANES), F32)
        both = picks(b)
        for h in range(2):
            row = pl.ds(2 * b + h, 1)
            values = jnp.concatenate(
                [
                    jnp.broadcast_to(hiv[row, :], (LANES, LANES)),
                    jnp.broadcast_to(lov[row, :], (LANES, LANES)),
                ],
                axis=0,
            ).astype(BF16)
            found = found + dot_nt(both[:, h * LANES:(h + 1) * LANES], values)
        high[b] = found[:, :LANES].astype(BF16)
        low[b] = jnp.where(found[:, LANES:] == lane_iota, 1.0, 0.0).astype(BF16)
        return carry

    lax.fori_loop(0, n_col, slot_step, 0, unroll=8)

    param_copy.wait()
    ptile = local_rows // 5

    def param_step(i, acc):
        block = pv_o[pl.ds(pl.multiple_of(i * ptile, 8), ptile), :]
        return acc + jnp.sum((block * block).reshape(ptile // 8, 8, LANES), axis=0)

    acc = lax.fori_loop(0, 5, param_step, jnp.zeros((8, LANES), F32))
    param_local = jnp.sum(jnp.sum(acc, axis=0, keepdims=True), axis=1, keepdims=True)

    grad[...] = jnp.zeros_like(grad)


    def parts(j):
        members = order[j * GROUP:(j + 1) * GROUP]
        arrivals = sum(1 for member in members if member != (0, 0))
        landed = recv.at[pl.ds(0, arrivals)]
        pltpu.make_async_copy(landed, landed, a2a_rsem.at[j]).wait()
        sources = [
            lax.rem(z + nz - dz, nz) * NX + lax.rem(x + NX - dx, NX) for dz, dx in members
        ]
        turned = jnp.concatenate([recv[src] for src in sources], axis=0).T
        hi = jnp.concatenate([high[src] for src in sources], axis=0)
        lo = jnp.concatenate([low[src] for src in sources], axis=0)
        zero = jnp.zeros_like(lo)
        for i in range(n_col // 2):
            onehot = jnp.concatenate(
                [jnp.where(hi == jnp.asarray(2 * i + h + 1, BF16), lo, zero) for h in range(2)], axis=1
            )
            part = dot(turned, onehot)
            for h in range(2):
                yield 2 * i + h, part[:, h * LANES:(h + 1) * LANES]

    last = n_col // GROUP - 1
    for j in range(last):
        for i, part in parts(j):
            grad[i] += part
    acc = jnp.zeros((LANES, LANES), F32)
    for i, part in parts(last):
        value = grad[i] + part
        grad[i] = value
        value = value * value
        acc = acc + value
        rs_send[i // nz, pl.ds(i % nz, 1), :] = jnp.sum(value, axis=0, keepdims=True)

    def exchange(src, dst, me, axis, q):
        for k in range(1, {"row": n_row, "x": NX, "col": n_col}[axis]):
            if axis == "row":
                device = {"row": lax.rem(r + k, n_row)}
                quarter = 0
            elif axis == "x":
                quarter = lax.rem(x + k, NX)
                device = {"col": z * NX + quarter}
            else:
                dz, dx = order[k - 1]
                quarter = lax.rem(x + dx, NX)
                device = {"col": lax.rem(z + dz, nz) * NX + quarter}
            pltpu.make_async_remote_copy(
                src_ref=src.at[quarter if src.shape[0] > 1 else 0], dst_ref=dst.at[me],
                send_sem=ssem.at[q], recv_sem=rsem.at[q],
                device_id=device, device_id_type=MESH,
            ).start()

    def wait_all(buf, q):
        rest = buf.at[pl.ds(0, buf.shape[0] - 1)]
        pltpu.make_async_copy(rest, rest, rsem.at[q]).wait()

    def sent_all(buf, sem):
        rest = buf.at[pl.ds(0, buf.shape[0] - 1)]
        pltpu.make_async_remote_copy(
            src_ref=rest, dst_ref=rest, send_sem=sem, recv_sem=sem,
            device_id={"row": lax.rem(r + 1, n_row)}, device_id_type=MESH,
        ).wait_send()

    col_send[0] = jnp.sum(acc.T, axis=0, keepdims=True)
    exchange(col_send, col_recv, r, "row", 0)
    exchange(rs_send, rs_recv, c, "col", 1)
    rs_recv[c] = rs_send[x]
    col_recv[r] = col_send[0]
    colm_copy.wait()
    rowm_copy.wait()
    for i in range(n_col):
        size = max(0, min(LANES, local_rows - i * LANES))
        if size < LANES:
            moments[pl.ds(i, 1), :] = jnp.ones((1, LANES), F32)
        if size:
            moments[i, :size] = rowm[pl.ds(i * LANES, size)]

    wait_all(col_recv, 0)
    col_total = jnp.sum(col_recv[...], axis=0)
    new_col = DECAY * colm[...] + (1.0 - DECAY) * (col_total / float(total_rows) + TINY)
    nc_o[...] = new_col
    turned_col = jnp.broadcast_to(new_col, (LANES, LANES)).T
    inverse_col = 1.0 / turned_col
    for i in range(n_col):
        value = grad[i]
        q_send[i // nz, pl.ds(i % nz, 1), :] = jnp.sum(value * value * inverse_col, axis=0, keepdims=True)
    exchange(q_send, q_recv, x, "x", 2)
    q_recv[x] = q_send[x]

    wait_all(rs_recv, 1)
    row_total = jnp.sum(rs_recv[...], axis=0)
    moment = moments[pl.ds(pl.multiple_of(x * nz, nz), nz), :]
    new_row = DECAY * moment + (1.0 - DECAY) * (row_total / float(total_cols) + TINY)
    ag_recv[x] = new_row
    exchange(ag_recv.at[pl.ds(x, 1)], ag_recv, x, "x", 3)
    wait_all(q_recv, 2)
    row_id = x * (nz * LANES) + iota((nz, LANES), 0) * LANES + iota((nz, LANES), 1)
    valid = row_id < local_rows
    raw_part = jnp.sum(q_recv[...], axis=0) / new_row

    def total_of(value):
        return jnp.sum(jnp.sum(jnp.where(valid, value, 0.0), axis=0, keepdims=True), axis=1, keepdims=True)

    lane = iota((1, LANES), 1)
    row_sum = total_of(new_row) * (1.0 / nz)
    raw_sum = total_of(raw_part)
    sc_send[0] = jnp.where(
        lane == 0, row_sum, jnp.where(lane == 1, raw_sum, jnp.where(lane == 2, param_local, 0.0))
    )
    exchange(sc_send, sc_recv, c, "col", 4)
    sc_recv[c] = sc_send[0]

    wait_all(ag_recv, 3)
    r_o[...] = ag_recv[...].reshape(n_col, LANES)
    col_rsqrt = lax.rsqrt(turned_col)

    def raw_chunk(i):
        size = min(LANES, local_rows - i * LANES)
        factor = lax.rsqrt(ag_recv[i // nz, pl.ds(i % nz, 1), :])
        raw_o[pl.ds(i * LANES, size), :] = (grad[i] * factor * col_rsqrt).T[:size]

    chunks = pl.cdiv(local_rows, LANES)
    for i in range(chunks // 2):
        raw_chunk(i)
    wait_all(sc_recv, 4)
    st_send[0] = jnp.sum(sc_recv[...], axis=0)
    exchange(st_send, st_recv, r, "row", 5)
    st_recv[r] = st_send[0]
    for i in range(chunks // 2, chunks):
        raw_chunk(i)
    wait_all(st_recv, 5)
    totals = jnp.sum(st_recv[...], axis=0)

    def pick_lane(k):
        return jnp.broadcast_to(
            jnp.sum(jnp.where(lane == k, totals, 0.0), axis=1, keepdims=True), (1, LANES)
        )

    mean_row = pick_lane(0) / float(total_rows)
    clip = jnp.maximum(1.0, jnp.sqrt(mean_row * pick_lane(1) / cells))
    root = jnp.sqrt(mean_row)
    step = RATE * jnp.sqrt(pick_lane(2) / cells)
    scal_o[0:1, :] = root / clip
    scal_o[1:2, :] = step
    scal_o[2:3, :] = root
    scal_o[3:8, :] = jnp.zeros((5, LANES), F32)

    sent_all(recv, a2a_ssem)
    for q, buf in enumerate((col_recv, rs_recv, q_recv, ag_recv, sc_recv, st_recv)):
        sent_all(buf, ssem.at[q])


def write_kernel(
    local_rows, raw, pv, rows, new_col, scal,
    np_o, up_o, nr_o, nc_o, rf_o,
    npv, upv, nrv, ncv, rfv, out_sem, small_sem,
):
    count = 10
    size = local_rows // count
    k = scal[0:1, :]
    step = scal[1:2, :]
    root = scal[2:3, :]
    copies = []
    for i in range(count):
        span = pl.ds(i * size, size)
        update = raw[span, :] * k
        upv[span, :] = update
        copies.append(pltpu.make_async_copy(upv.at[span], up_o.at[span], out_sem.at[0, i]))
        copies[-1].start()
        npv[span, :] = pv[span, :] - step * update
        copies.append(pltpu.make_async_copy(npv.at[span], np_o.at[span], out_sem.at[1, i]))
        copies[-1].start()
        if i == 0:
            values = rows[...]
            factor = lax.rsqrt(values) * root
            for j in range(pl.cdiv(local_rows, LANES)):
                n = min(LANES, local_rows - j * LANES)
                nrv[pl.ds(j * LANES, n)] = values[j, :n]
                rfv[pl.ds(j * LANES, n)] = factor[j, :n]
            ncv[...] = new_col[0, :]
            for q, (src, dst) in enumerate(((nrv, nr_o), (rfv, rf_o), (ncv, nc_o))):
                copies.append(pltpu.make_async_copy(src, dst, small_sem.at[q]))
                copies[-1].start()
    for copy in copies:
        copy.wait()


def body(n_row, n_col, cotangent, token_ids, param, row_moment, col_moment):
    local_rows, width = param.shape
    total_rows = local_rows * n_row
    total_cols = width * n_col
    nz = n_col // NX
    vmem = pl.BlockSpec(memory_space=pltpu.VMEM)
    hbm = pl.BlockSpec(memory_space=pltpu.HBM)
    dma = pltpu.SemaphoreType.DMA

    ids_shape = (n_col * BLOCK // LANES, LANES)

    def stay(value):
        return pltpu.with_memory_space_constraint(value, pltpu.HBM)

    raw, pv, rows, new_col, scal = pl.pallas_call(
        functools.partial(step_kernel, n_row, n_col, local_rows, total_rows, total_cols),
        out_shape=(
            pltpu.VMEM((local_rows, LANES), F32),
            pltpu.VMEM((local_rows, LANES), F32),
            pltpu.VMEM((n_col, LANES), F32),
            pltpu.VMEM((1, LANES), F32),
            pltpu.VMEM((8, LANES), F32),
        ),
        in_specs=[hbm] * 5,
        out_specs=(vmem,) * 5,
        scratch_shapes=[
            pltpu.VMEM((nz, BLOCK, NX * LANES), BF16),
            pltpu.VMEM(ids_shape, jnp.int32),
            pltpu.VMEM((local_rows,), F32),
            pltpu.VMEM((n_col, LANES), F32),
            pltpu.VMEM((1, LANES), F32),
            pltpu.VMEM(ids_shape, F32),
            pltpu.VMEM(ids_shape, F32),
            pltpu.VMEM(ids_shape, F32),
            pltpu.VMEM((n_col, CAP, LANES), BF16),
            pltpu.VMEM((n_col, CAP, LANES), BF16),
            pltpu.VMEM((nz, NX, CAP, LANES), BF16),
            pltpu.VMEM((n_col, CAP, LANES), BF16),
            pltpu.VMEM((n_col, LANES, LANES), F32),
            pltpu.VMEM((1, 1, LANES), F32),
            pltpu.VMEM((n_row, 1, LANES), F32),
            pltpu.VMEM((NX, nz, LANES), F32),
            pltpu.VMEM((n_col, nz, LANES), F32),
            pltpu.VMEM((NX, nz, LANES), F32),
            pltpu.VMEM((NX, nz, LANES), F32),
            pltpu.VMEM((NX, nz, LANES), F32),
            pltpu.VMEM((1, 1, LANES), F32),
            pltpu.VMEM((n_col, 1, LANES), F32),
            pltpu.VMEM((1, 1, LANES), F32),
            pltpu.VMEM((n_row, 1, LANES), F32),
            dma((4,)),
            dma((nz,)),
            dma,
            dma((n_col // GROUP,)),
            dma((6,)),
            dma((6,)),
        ],
        compiler_params=pltpu.CompilerParams(
            collective_id=0, has_side_effects=True, vmem_limit_bytes=32 * 1024 * 1024
        ),
        name="adafactor_step",
    )(
        stay(cotangent), stay(token_ids.reshape(ids_shape)), stay(param), stay(row_moment),
        stay(col_moment.reshape(1, LANES)),
    )

    return pl.pallas_call(
        functools.partial(write_kernel, local_rows),
        out_shape=(
            jax.ShapeDtypeStruct((local_rows, LANES), F32),
            jax.ShapeDtypeStruct((local_rows, LANES), F32),
            jax.ShapeDtypeStruct((local_rows,), F32),
            jax.ShapeDtypeStruct((LANES,), F32),
            jax.ShapeDtypeStruct((local_rows,), F32),
        ),
        in_specs=[vmem] * 5,
        out_specs=(hbm,) * 5,
        scratch_shapes=[
            pltpu.VMEM((local_rows, LANES), F32),
            pltpu.VMEM((local_rows, LANES), F32),
            pltpu.VMEM((local_rows,), F32),
            pltpu.VMEM((LANES,), F32),
            pltpu.VMEM((local_rows,), F32),
            dma((2, 10)),
            dma((3,)),
        ],
        compiler_params=pltpu.CompilerParams(vmem_limit_bytes=16 * 1024 * 1024),
        name="adafactor_write",
    )(raw, pv, rows, new_col, scal)


def solution(mesh):
    n_row, n_col = mesh.shape["row"], mesh.shape["col"]
    in_specs = (P("col", None), P(), P("row", "col"), P("row"), P("col"))
    out_specs = (P("row", "col"), P("row", "col"), P("row"), P("col"), P("row"))
    return jax.shard_map(
        functools.partial(body, n_row, n_col),
        mesh=mesh, in_specs=in_specs, out_specs=out_specs, check_vma=False,
    )
```

```python
import functools

import jax
import jax.numpy as jnp
from jax import lax
from jax.experimental import pallas as pl
from jax.experimental.pallas import tpu as pltpu
from jax.sharding import PartitionSpec as P

STEP = 100
DECAY = 1.0 - STEP ** (-0.8)
RATE = min(0.01, STEP ** (-0.5))
TINY = 1e-30
CAP = 64
BLOCK = 256
LANES = 128
NX = 4
GROUP = 4
MESH = pl.DeviceIdType.MESH
F32 = jnp.float32
BF16 = jnp.bfloat16


def iota(shape, dim):
    return lax.broadcasted_iota(jnp.int32, shape, dim)


def dot(a, b):
    return jnp.dot(a, b, preferred_element_type=F32)


def dot_nt(a, b):
    return lax.dot_general(a, b, (((1,), (1,)), ((), ())), preferred_element_type=F32)


def order_of(nz):
    far = sorted(range(nz), key=lambda d: (-min(d, nz - d), d))
    return [(dz, dx) for dx in (2, 1, 3, 0) for dz in far]


def step_kernel(
    n_row, n_col, local_rows, total_rows, total_cols,
    cot, ids_hbm, param, rowm_hbm, colm_hbm,
    raw_o, pv_o, r_o, nc_o, scal_o,
    cotv, ids, rowm, moments, colm, posv, hiv, lov, high, low, send, recv, grad,
    col_send, col_recv, rs_send, rs_recv, q_send, q_recv,
    ag_recv, pair, chips,
    in_sem, cot_sem, a2a_ssem, a2a_rsem, ssem, rsem,
):
    nz = n_col // NX
    cells = float(total_rows) * float(total_cols)
    width = NX * LANES
    r = lax.axis_index("row")
    c = lax.axis_index("col")
    z = c // NX
    x = lax.rem(c, NX)
    y = r // 2
    core = lax.rem(r, 2)
    ny = n_row // 2
    order = order_of(nz)

    barrier = pltpu.get_barrier_semaphore()
    for dz, dx in order[:-1]:
        peer = lax.rem(z + dz, nz) * NX + lax.rem(x + dx, NX)
        pl.semaphore_signal(barrier, inc=1, device_id={"col": peer}, device_id_type=MESH)
    for k in range(1, n_row):
        pl.semaphore_signal(
            barrier, inc=1, device_id={"row": lax.rem(r + k, n_row)}, device_id_type=MESH
        )

    ids_copy = pltpu.make_async_copy(ids_hbm, ids, in_sem.at[0])
    ids_copy.start()

    def cot_copy(j):
        zt = lax.rem(z + j, nz)
        return pltpu.make_async_copy(
            cot.at[:, pl.ds(pl.multiple_of(zt * width, width), width)], cotv.at[j], cot_sem.at[j]
        )

    for j in range(nz):
        cot_copy(j).start()

    rowm_copy = pltpu.make_async_copy(rowm_hbm, rowm, in_sem.at[1])
    rowm_copy.start()
    colm_copy = pltpu.make_async_copy(colm_hbm, colm, in_sem.at[2])
    colm_copy.start()
    param_copy = pltpu.make_async_copy(param, pv_o, in_sem.at[3])
    param_copy.start()

    ids_copy.wait()
    local = ids[...] - r * local_rows
    inside = (local >= 0) & (local < local_rows)
    ones = jnp.where(inside, 1.0, 0.0).astype(BF16)
    before = jnp.where(iota((LANES, LANES), 0) < iota((LANES, LANES), 1), 1.0, 0.0).astype(BF16)
    count = dot(ones, before)
    total = dot(ones, jnp.ones((LANES, LANES), BF16))
    odd = lax.rem(iota(local.shape, 0), 2) == 1
    position = count + jnp.where(odd, pltpu.roll(total, 1, 0), 0.0)
    posv[...] = jnp.where(inside, position, -1000.0)
    hiv[...] = jnp.where(inside, (local >> 7) + 1, 0).astype(F32)
    lov[...] = jnp.where(inside, local & 127, 0).astype(F32)

    slot_iota = iota((CAP, LANES), 0).astype(F32)

    def picks(block):
        return jnp.concatenate(
            [
                jnp.where(posv[pl.ds(2 * block + h, 1), :] == slot_iota, 1.0, 0.0).astype(BF16)
                for h in range(2)
            ],
            axis=1,
        )

    pick = picks(c)

    for j in range(nz):
        cot_copy(j).wait()
        packed = dot(pick, cotv[j]).astype(BF16)
        for k in range(NX):
            send[j, k] = packed[:, k * LANES:(k + 1) * LANES]
    recv[c] = send[0, x]
    pl.semaphore_wait(barrier, n_col + n_row - 2)
    for n, (dz, dx) in enumerate(order[:-1]):
        xt = lax.rem(x + dx, NX)
        pltpu.make_async_remote_copy(
            src_ref=send.at[dz, xt], dst_ref=recv.at[c],
            send_sem=a2a_ssem, recv_sem=a2a_rsem.at[n // GROUP],
            device_id={"col": lax.rem(z + dz, nz) * NX + xt}, device_id_type=MESH,
        ).start()

    lane_iota = iota((CAP, LANES), 1).astype(F32)

    def slot_step(b, carry):
        found = jnp.zeros((CAP, 2 * LANES), F32)
        both = picks(b)
        for h in range(2):
            row = pl.ds(2 * b + h, 1)
            values = jnp.concatenate(
                [
                    jnp.broadcast_to(hiv[row, :], (LANES, LANES)),
                    jnp.broadcast_to(lov[row, :], (LANES, LANES)),
                ],
                axis=0,
            ).astype(BF16)
            found = found + dot_nt(both[:, h * LANES:(h + 1) * LANES], values)
        high[b] = found[:, :LANES].astype(BF16)
        low[b] = jnp.where(found[:, LANES:] == lane_iota, 1.0, 0.0).astype(BF16)
        return carry

    lax.fori_loop(0, n_col, slot_step, 0, unroll=8)

    param_copy.wait()
    ptile = local_rows // 5

    def param_step(i, acc):
        block = pv_o[pl.ds(pl.multiple_of(i * ptile, 8), ptile), :]
        return acc + jnp.sum((block * block).reshape(ptile // 8, 8, LANES), axis=0)

    acc = lax.fori_loop(0, 5, param_step, jnp.zeros((8, LANES), F32))
    param_local = jnp.sum(jnp.sum(acc, axis=0, keepdims=True), axis=1, keepdims=True)

    grad[...] = jnp.zeros_like(grad)


    def parts(j):
        members = order[j * GROUP:(j + 1) * GROUP]
        arrivals = sum(1 for member in members if member != (0, 0))
        landed = recv.at[pl.ds(0, arrivals)]
        pltpu.make_async_copy(landed, landed, a2a_rsem.at[j]).wait()
        sources = [
            lax.rem(z + nz - dz, nz) * NX + lax.rem(x + NX - dx, NX) for dz, dx in members
        ]
        turned = jnp.concatenate([recv[src] for src in sources], axis=0).T
        hi = jnp.concatenate([high[src] for src in sources], axis=0)
        lo = jnp.concatenate([low[src] for src in sources], axis=0)
        zero = jnp.zeros_like(lo)
        for i in range(n_col // 2):
            onehot = jnp.concatenate(
                [jnp.where(hi == jnp.asarray(2 * i + h + 1, BF16), lo, zero) for h in range(2)], axis=1
            )
            part = dot(turned, onehot)
            for h in range(2):
                yield 2 * i + h, part[:, h * LANES:(h + 1) * LANES]

    last = n_col // GROUP - 1
    for j in range(last):
        for i, part in parts(j):
            grad[i] += part
    acc = jnp.zeros((LANES, LANES), F32)
    for i, part in parts(last):
        value = grad[i] + part
        grad[i] = value
        value = value * value
        acc = acc + value
        rs_send[i // nz, pl.ds(i % nz, 1), :] = jnp.sum(value, axis=0, keepdims=True)

    def exchange(src, dst, me, axis, q):
        for k in range(1, {"row": n_row, "x": NX, "col": n_col}[axis]):
            if axis == "row":
                device = {"row": lax.rem(r + k, n_row)}
                quarter = 0
            elif axis == "x":
                quarter = lax.rem(x + k, NX)
                device = {"col": z * NX + quarter}
            else:
                dz, dx = order[k - 1]
                quarter = lax.rem(x + dx, NX)
                device = {"col": lax.rem(z + dz, nz) * NX + quarter}
            pltpu.make_async_remote_copy(
                src_ref=src.at[quarter if src.shape[0] > 1 else 0], dst_ref=dst.at[me],
                send_sem=ssem.at[q], recv_sem=rsem.at[q],
                device_id=device, device_id_type=MESH,
            ).start()

    def wait_all(buf, q):
        rest = buf.at[pl.ds(0, buf.shape[0] - 1)]
        pltpu.make_async_copy(rest, rest, rsem.at[q]).wait()

    def sent_all(buf, sem):
        rest = buf.at[pl.ds(0, buf.shape[0] - 1)]
        pltpu.make_async_remote_copy(
            src_ref=rest, dst_ref=rest, send_sem=sem, recv_sem=sem,
            device_id={"row": lax.rem(r + 1, n_row)}, device_id_type=MESH,
        ).wait_send()

    col_send[0] = jnp.sum(acc.T, axis=0, keepdims=True)
    exchange(col_send, col_recv, r, "row", 0)
    exchange(rs_send, rs_recv, c, "col", 1)
    rs_recv[c] = rs_send[x]
    col_recv[r] = col_send[0]
    colm_copy.wait()
    rowm_copy.wait()
    for i in range(n_col):
        size = max(0, min(LANES, local_rows - i * LANES))
        if size < LANES:
            moments[pl.ds(i, 1), :] = jnp.ones((1, LANES), F32)
        if size:
            moments[i, :size] = rowm[pl.ds(i * LANES, size)]

    wait_all(col_recv, 0)
    col_total = jnp.sum(col_recv[...], axis=0)
    new_col = DECAY * colm[...] + (1.0 - DECAY) * (col_total / float(total_rows) + TINY)
    nc_o[...] = new_col
    turned_col = jnp.broadcast_to(new_col, (LANES, LANES)).T
    inverse_col = 1.0 / turned_col
    for i in range(n_col):
        value = grad[i]
        q_send[i // nz, pl.ds(i % nz, 1), :] = jnp.sum(value * value * inverse_col, axis=0, keepdims=True)
    exchange(q_send, q_recv, x, "x", 2)
    q_recv[x] = q_send[x]

    wait_all(rs_recv, 1)
    row_total = jnp.sum(rs_recv[...], axis=0)
    moment = moments[pl.ds(pl.multiple_of(x * nz, nz), nz), :]
    new_row = DECAY * moment + (1.0 - DECAY) * (row_total / float(total_cols) + TINY)
    ag_recv[x] = new_row
    exchange(ag_recv.at[pl.ds(x, 1)], ag_recv, x, "x", 3)
    wait_all(q_recv, 2)
    row_id = x * (nz * LANES) + iota((nz, LANES), 0) * LANES + iota((nz, LANES), 1)
    valid = row_id < local_rows
    raw_part = jnp.sum(q_recv[...], axis=0) / new_row

    def total_of(value):
        return jnp.sum(jnp.sum(jnp.where(valid, value, 0.0), axis=0, keepdims=True), axis=1, keepdims=True)

    lane = iota((1, LANES), 1)
    row_sum = total_of(new_row) * (1.0 / nz)
    raw_sum = total_of(raw_part)
    pair[core] = jnp.where(
        lane == 0, row_sum, jnp.where(lane == 1, raw_sum, jnp.where(lane == 2, param_local, 0.0))
    )
    pltpu.make_async_remote_copy(
        src_ref=pair.at[core], dst_ref=pair.at[core], send_sem=ssem.at[4], recv_sem=rsem.at[4],
        device_id={"row": 2 * y + 1 - core}, device_id_type=MESH,
    ).start()
    wait_all(pair, 4)
    chip = c * ny + y
    chips[chip] = pair[0] + pair[1]
    for dz, dx in order:
        for dy in range(ny - 1, -1, -1):
            if dz or dx or dy:
                to_row = 2 * lax.rem(y + dy, ny) + core
                to_col = lax.rem(z + dz, nz) * NX + lax.rem(x + dx, NX)
                pltpu.make_async_remote_copy(
                    src_ref=chips.at[chip], dst_ref=chips.at[chip],
                    send_sem=ssem.at[5], recv_sem=rsem.at[5],
                    device_id={"row": to_row, "col": to_col}, device_id_type=MESH,
                ).start()

    wait_all(ag_recv, 3)
    r_o[...] = ag_recv[...].reshape(n_col, LANES)
    col_rsqrt = lax.rsqrt(turned_col)

    def raw_chunk(i):
        size = min(LANES, local_rows - i * LANES)
        factor = lax.rsqrt(ag_recv[i // nz, pl.ds(i % nz, 1), :])
        raw_o[pl.ds(i * LANES, size), :] = (grad[i] * factor * col_rsqrt).T[:size]

    for i in range(pl.cdiv(local_rows, LANES)):
        raw_chunk(i)
    wait_all(chips, 5)
    totals = jnp.sum(chips[...], axis=0)

    def pick_lane(k):
        return jnp.broadcast_to(
            jnp.sum(jnp.where(lane == k, totals, 0.0), axis=1, keepdims=True), (1, LANES)
        )

    mean_row = pick_lane(0) / float(total_rows)
    clip = jnp.maximum(1.0, jnp.sqrt(mean_row * pick_lane(1) / cells))
    root = jnp.sqrt(mean_row)
    step = RATE * jnp.sqrt(pick_lane(2) / cells)
    scal_o[0:1, :] = root / clip
    scal_o[1:2, :] = step
    scal_o[2:3, :] = root
    scal_o[3:8, :] = jnp.zeros((5, LANES), F32)

    sent_all(recv, a2a_ssem)
    for q, buf in enumerate((col_recv, rs_recv, q_recv, ag_recv, pair, chips)):
        sent_all(buf, ssem.at[q])


def write_kernel(
    local_rows, raw, pv, rows, new_col, scal,
    np_o, up_o, nr_o, nc_o, rf_o,
    npv, upv, nrv, ncv, rfv, out_sem, small_sem,
):
    count = 10
    size = local_rows // count
    k = scal[0:1, :]
    step = scal[1:2, :]
    root = scal[2:3, :]
    copies = []
    for i in range(count):
        span = pl.ds(i * size, size)
        update = raw[span, :] * k
        upv[span, :] = update
        copies.append(pltpu.make_async_copy(upv.at[span], up_o.at[span], out_sem.at[0, i]))
        copies[-1].start()
        npv[span, :] = pv[span, :] - step * update
        copies.append(pltpu.make_async_copy(npv.at[span], np_o.at[span], out_sem.at[1, i]))
        copies[-1].start()
        if i == 0:
            values = rows[...]
            factor = lax.rsqrt(values) * root
            for j in range(pl.cdiv(local_rows, LANES)):
                n = min(LANES, local_rows - j * LANES)
                nrv[pl.ds(j * LANES, n)] = values[j, :n]
                rfv[pl.ds(j * LANES, n)] = factor[j, :n]
            ncv[...] = new_col[0, :]
            for q, (src, dst) in enumerate(((nrv, nr_o), (rfv, rf_o), (ncv, nc_o))):
                copies.append(pltpu.make_async_copy(src, dst, small_sem.at[q]))
                copies[-1].start()
    for copy in copies:
        copy.wait()


def body(n_row, n_col, cotangent, token_ids, param, row_moment, col_moment):
    local_rows, width = param.shape
    total_rows = local_rows * n_row
    total_cols = width * n_col
    nz = n_col // NX
    vmem = pl.BlockSpec(memory_space=pltpu.VMEM)
    hbm = pl.BlockSpec(memory_space=pltpu.HBM)
    dma = pltpu.SemaphoreType.DMA

    ids_shape = (n_col * BLOCK // LANES, LANES)

    def stay(value):
        return pltpu.with_memory_space_constraint(value, pltpu.HBM)

    raw, pv, rows, new_col, scal = pl.pallas_call(
        functools.partial(step_kernel, n_row, n_col, local_rows, total_rows, total_cols),
        out_shape=(
            pltpu.VMEM((local_rows, LANES), F32),
            pltpu.VMEM((local_rows, LANES), F32),
            pltpu.VMEM((n_col, LANES), F32),
            pltpu.VMEM((1, LANES), F32),
            pltpu.VMEM((8, LANES), F32),
        ),
        in_specs=[hbm] * 5,
        out_specs=(vmem,) * 5,
        scratch_shapes=[
            pltpu.VMEM((nz, BLOCK, NX * LANES), BF16),
            pltpu.VMEM(ids_shape, jnp.int32),
            pltpu.VMEM((local_rows,), F32),
            pltpu.VMEM((n_col, LANES), F32),
            pltpu.VMEM((1, LANES), F32),
            pltpu.VMEM(ids_shape, F32),
            pltpu.VMEM(ids_shape, F32),
            pltpu.VMEM(ids_shape, F32),
            pltpu.VMEM((n_col, CAP, LANES), BF16),
            pltpu.VMEM((n_col, CAP, LANES), BF16),
            pltpu.VMEM((nz, NX, CAP, LANES), BF16),
            pltpu.VMEM((n_col, CAP, LANES), BF16),
            pltpu.VMEM((n_col, LANES, LANES), F32),
            pltpu.VMEM((1, 1, LANES), F32),
            pltpu.VMEM((n_row, 1, LANES), F32),
            pltpu.VMEM((NX, nz, LANES), F32),
            pltpu.VMEM((n_col, nz, LANES), F32),
            pltpu.VMEM((NX, nz, LANES), F32),
            pltpu.VMEM((NX, nz, LANES), F32),
            pltpu.VMEM((NX, nz, LANES), F32),
            pltpu.VMEM((2, 1, LANES), F32),
            pltpu.VMEM((n_col * n_row // 2, 1, LANES), F32),
            dma((4,)),
            dma((nz,)),
            dma,
            dma((n_col // GROUP,)),
            dma((6,)),
            dma((6,)),
        ],
        compiler_params=pltpu.CompilerParams(
            collective_id=0, has_side_effects=True, vmem_limit_bytes=32 * 1024 * 1024
        ),
        name="adafactor_step",
    )(
        stay(cotangent), stay(token_ids.reshape(ids_shape)), stay(param), stay(row_moment),
        stay(col_moment.reshape(1, LANES)),
    )

    return pl.pallas_call(
        functools.partial(write_kernel, local_rows),
        out_shape=(
            jax.ShapeDtypeStruct((local_rows, LANES), F32),
            jax.ShapeDtypeStruct((local_rows, LANES), F32),
            jax.ShapeDtypeStruct((local_rows,), F32),
            jax.ShapeDtypeStruct((LANES,), F32),
            jax.ShapeDtypeStruct((local_rows,), F32),
        ),
        in_specs=[vmem] * 5,
        out_specs=(hbm,) * 5,
        scratch_shapes=[
            pltpu.VMEM((local_rows, LANES), F32),
            pltpu.VMEM((local_rows, LANES), F32),
            pltpu.VMEM((local_rows,), F32),
            pltpu.VMEM((LANES,), F32),
            pltpu.VMEM((local_rows,), F32),
            dma((2, 10)),
            dma((3,)),
        ],
        compiler_params=pltpu.CompilerParams(vmem_limit_bytes=16 * 1024 * 1024),
        name="adafactor_write",
    )(raw, pv, rows, new_col, scal)


def solution(mesh):
    n_row, n_col = mesh.shape["row"], mesh.shape["col"]
    in_specs = (P("col", None), P(), P("row", "col"), P("row"), P("col"))
    out_specs = (P("row", "col"), P("row", "col"), P("row"), P("col"), P("row"))
    return jax.shard_map(
        functools.partial(body, n_row, n_col),
        mesh=mesh, in_specs=in_specs, out_specs=out_specs, check_vma=False,
    )
```

```python
import functools

import jax
import jax.numpy as jnp
from jax import lax
from jax.experimental import pallas as pl
from jax.experimental.pallas import tpu as pltpu
from jax.sharding import PartitionSpec as P

STEP = 100
DECAY = 1.0 - STEP ** (-0.8)
RATE = min(0.01, STEP ** (-0.5))
TINY = 1e-30
CAP = 64
BLOCK = 256
LANES = 128
NX = 4
GROUP = 4
MESH = pl.DeviceIdType.MESH
F32 = jnp.float32
BF16 = jnp.bfloat16


def iota(shape, dim):
    return lax.broadcasted_iota(jnp.int32, shape, dim)


def dot(a, b):
    return jnp.dot(a, b, preferred_element_type=F32)


def dot_nt(a, b):
    return lax.dot_general(a, b, (((1,), (1,)), ((), ())), preferred_element_type=F32)


def order_of(nz):
    far = sorted(range(nz), key=lambda d: (-min(d, nz - d), d))
    return [(dz, dx) for dx in (2, 1, 3, 0) for dz in far]


def step_kernel(
    n_row, n_col, local_rows, total_rows, total_cols,
    cot, ids_hbm, param, rowm_hbm, colm_hbm,
    raw_o, pv_o, r_o, nc_o, scal_o,
    cotv, ids, rowm, moments, colm, posv, hiv, lov, high, low, ready, send, recv, grad,
    col_send, col_recv, rs_send, rs_recv, q_send, q_recv,
    ag_recv, pair, chips,
    in_sem, cot_sem, a2a_ssem, a2a_rsem, ssem, rsem,
):
    nz = n_col // NX
    cells = float(total_rows) * float(total_cols)
    width = NX * LANES
    r = lax.axis_index("row")
    c = lax.axis_index("col")
    z = c // NX
    x = lax.rem(c, NX)
    y = r // 2
    core = lax.rem(r, 2)
    ny = n_row // 2
    order = order_of(nz)

    barrier = pltpu.get_barrier_semaphore()
    for dz, dx in order[:-1]:
        peer = lax.rem(z + dz, nz) * NX + lax.rem(x + dx, NX)
        pl.semaphore_signal(barrier, inc=1, device_id={"col": peer}, device_id_type=MESH)
    for k in range(1, n_row):
        pl.semaphore_signal(
            barrier, inc=1, device_id={"row": lax.rem(r + k, n_row)}, device_id_type=MESH
        )

    ids_copy = pltpu.make_async_copy(ids_hbm, ids, in_sem.at[0])
    ids_copy.start()

    def cot_copy(j):
        zt = lax.rem(z + j, nz)
        return pltpu.make_async_copy(
            cot.at[:, pl.ds(pl.multiple_of(zt * width, width), width)], cotv.at[j], cot_sem
        )

    for j in range(nz):
        cot_copy(j).start()

    rowm_copy = pltpu.make_async_copy(rowm_hbm, rowm, in_sem.at[1])
    rowm_copy.start()
    colm_copy = pltpu.make_async_copy(colm_hbm, colm, in_sem.at[2])
    colm_copy.start()
    param_copy = pltpu.make_async_copy(param, pv_o, in_sem.at[3])
    param_copy.start()

    ids_copy.wait()
    local = ids[...] - r * local_rows
    inside = (local >= 0) & (local < local_rows)
    ones = jnp.where(inside, 1.0, 0.0).astype(BF16)
    before = jnp.where(iota((LANES, LANES), 0) < iota((LANES, LANES), 1), 1.0, 0.0).astype(BF16)
    count = dot(ones, before)
    total = dot(ones, jnp.ones((LANES, LANES), BF16))
    odd = lax.rem(iota(local.shape, 0), 2) == 1
    position = count + jnp.where(odd, pltpu.roll(total, 1, 0), 0.0)
    posv[...] = jnp.where(inside, position, -1000.0)
    hiv[...] = jnp.where(inside, (local >> 7) + 1, 0).astype(F32)
    lov[...] = jnp.where(inside, local & 127, 0).astype(F32)

    slot_iota = iota((CAP, LANES), 0).astype(F32)

    def picks(block):
        return jnp.concatenate(
            [
                jnp.where(posv[pl.ds(2 * block + h, 1), :] == slot_iota, 1.0, 0.0).astype(BF16)
                for h in range(2)
            ],
            axis=1,
        )

    pick = picks(c)

    pltpu.make_async_copy(cotv, cotv, cot_sem).wait()
    for j in range(nz):
        packed = dot(pick, cotv[j]).astype(BF16)
        for k in range(NX):
            send[j, k] = packed[:, k * LANES:(k + 1) * LANES]
    recv[c] = send[0, x]
    pl.semaphore_wait(barrier, n_col + n_row - 2)
    for n, (dz, dx) in enumerate(order[:-1]):
        xt = lax.rem(x + dx, NX)
        pltpu.make_async_remote_copy(
            src_ref=send.at[dz, xt], dst_ref=recv.at[c],
            send_sem=a2a_ssem, recv_sem=a2a_rsem.at[n // GROUP],
            device_id={"col": lax.rem(z + dz, nz) * NX + xt}, device_id_type=MESH,
        ).start()

    lane_iota = iota((CAP, LANES), 1).astype(F32)

    def slot_step(b, carry):
        found = jnp.zeros((CAP, 2 * LANES), F32)
        both = picks(b)
        for h in range(2):
            row = pl.ds(2 * b + h, 1)
            values = jnp.concatenate(
                [
                    jnp.broadcast_to(hiv[row, :], (LANES, LANES)),
                    jnp.broadcast_to(lov[row, :], (LANES, LANES)),
                ],
                axis=0,
            ).astype(BF16)
            found = found + dot_nt(both[:, h * LANES:(h + 1) * LANES], values)
        high[b] = found[:, :LANES].astype(BF16)
        low[b] = jnp.where(found[:, LANES:] == lane_iota, 1.0, 0.0).astype(BF16)
        return carry

    lax.fori_loop(0, n_col, slot_step, 0, unroll=8)

    param_copy.wait()
    ptile = local_rows // 5

    def param_step(i, acc):
        block = pv_o[pl.ds(pl.multiple_of(i * ptile, 8), ptile), :]
        return acc + jnp.sum((block * block).reshape(ptile // 8, 8, LANES), axis=0)

    acc = lax.fori_loop(0, 5, param_step, jnp.zeros((8, LANES), F32))
    param_local = jnp.sum(jnp.sum(acc, axis=0, keepdims=True), axis=1, keepdims=True)

    grad[...] = jnp.zeros_like(grad)


    last = n_col // GROUP - 1
    kept = range(max(0, last - 1), last + 1)

    def sources(j):
        return [
            lax.rem(z + nz - dz, nz) * NX + lax.rem(x + NX - dx, NX)
            for dz, dx in order[j * GROUP:(j + 1) * GROUP]
        ]

    def onehots(j):
        hi = jnp.concatenate([high[src] for src in sources(j)], axis=0)
        lo = jnp.concatenate([low[src] for src in sources(j)], axis=0)
        zero = jnp.zeros_like(lo)
        for i in range(n_col // 2):
            yield jnp.concatenate(
                [jnp.where(hi == jnp.asarray(2 * i + h + 1, BF16), lo, zero) for h in range(2)], axis=1
            )

    for j in kept:
        for i, onehot in enumerate(onehots(j)):
            ready[j - kept[0], i] = onehot

    def parts(j):
        arrivals = sum(1 for member in order[j * GROUP:(j + 1) * GROUP] if member != (0, 0))
        landed = recv.at[pl.ds(0, arrivals)]
        pltpu.make_async_copy(landed, landed, a2a_rsem.at[j]).wait()
        turned = jnp.concatenate([recv[src] for src in sources(j)], axis=0).T
        made = (ready[j - kept[0], i] for i in range(n_col // 2)) if j in kept else onehots(j)
        for i, onehot in enumerate(made):
            part = dot(turned, onehot)
            for h in range(2):
                yield 2 * i + h, part[:, h * LANES:(h + 1) * LANES]

    for j in range(last):
        for i, part in parts(j):
            grad[i] += part
    acc = jnp.zeros((LANES, LANES), F32)
    for i, part in parts(last):
        value = grad[i] + part
        grad[i] = value
        value = value * value
        acc = acc + value
        rs_send[i // nz, pl.ds(i % nz, 1), :] = jnp.sum(value, axis=0, keepdims=True)

    def exchange(src, dst, me, axis, q):
        for k in range(1, {"row": n_row, "x": NX, "col": n_col}[axis]):
            if axis == "row":
                device = {"row": lax.rem(r + k, n_row)}
                quarter = 0
            elif axis == "x":
                quarter = lax.rem(x + k, NX)
                device = {"col": z * NX + quarter}
            else:
                dz, dx = order[k - 1]
                quarter = lax.rem(x + dx, NX)
                device = {"col": lax.rem(z + dz, nz) * NX + quarter}
            pltpu.make_async_remote_copy(
                src_ref=src.at[quarter if src.shape[0] > 1 else 0], dst_ref=dst.at[me],
                send_sem=ssem.at[q], recv_sem=rsem.at[q],
                device_id=device, device_id_type=MESH,
            ).start()

    def wait_all(buf, q):
        rest = buf.at[pl.ds(0, buf.shape[0] - 1)]
        pltpu.make_async_copy(rest, rest, rsem.at[q]).wait()

    def sent_all(buf, sem):
        rest = buf.at[pl.ds(0, buf.shape[0] - 1)]
        pltpu.make_async_remote_copy(
            src_ref=rest, dst_ref=rest, send_sem=sem, recv_sem=sem,
            device_id={"row": lax.rem(r + 1, n_row)}, device_id_type=MESH,
        ).wait_send()

    col_send[0] = jnp.sum(acc.T, axis=0, keepdims=True)
    exchange(col_send, col_recv, r, "row", 0)
    exchange(rs_send, rs_recv, c, "col", 1)
    rs_recv[c] = rs_send[x]
    col_recv[r] = col_send[0]
    colm_copy.wait()
    rowm_copy.wait()
    for i in range(n_col):
        size = max(0, min(LANES, local_rows - i * LANES))
        if size < LANES:
            moments[pl.ds(i, 1), :] = jnp.ones((1, LANES), F32)
        if size:
            moments[i, :size] = rowm[pl.ds(i * LANES, size)]

    wait_all(col_recv, 0)
    col_total = jnp.sum(col_recv[...], axis=0)
    new_col = DECAY * colm[...] + (1.0 - DECAY) * (col_total / float(total_rows) + TINY)
    nc_o[...] = new_col
    turned_col = jnp.broadcast_to(new_col, (LANES, LANES)).T
    inverse_col = 1.0 / turned_col
    for i in range(n_col):
        value = grad[i]
        q_send[i // nz, pl.ds(i % nz, 1), :] = jnp.sum(value * value * inverse_col, axis=0, keepdims=True)
    exchange(q_send, q_recv, x, "x", 2)
    q_recv[x] = q_send[x]

    wait_all(rs_recv, 1)
    row_total = jnp.sum(rs_recv[...], axis=0)
    moment = moments[pl.ds(pl.multiple_of(x * nz, nz), nz), :]
    new_row = DECAY * moment + (1.0 - DECAY) * (row_total / float(total_cols) + TINY)
    ag_recv[x] = new_row
    exchange(ag_recv.at[pl.ds(x, 1)], ag_recv, x, "x", 3)
    wait_all(q_recv, 2)
    row_id = x * (nz * LANES) + iota((nz, LANES), 0) * LANES + iota((nz, LANES), 1)
    valid = row_id < local_rows
    raw_part = jnp.sum(q_recv[...], axis=0) / new_row

    def total_of(value):
        return jnp.sum(jnp.sum(jnp.where(valid, value, 0.0), axis=0, keepdims=True), axis=1, keepdims=True)

    lane = iota((1, LANES), 1)
    row_sum = total_of(new_row) * (1.0 / nz)
    raw_sum = total_of(raw_part)
    pair[core] = jnp.where(
        lane == 0, row_sum, jnp.where(lane == 1, raw_sum, jnp.where(lane == 2, param_local, 0.0))
    )
    pltpu.make_async_remote_copy(
        src_ref=pair.at[core], dst_ref=pair.at[core], send_sem=ssem.at[4], recv_sem=rsem.at[4],
        device_id={"row": 2 * y + 1 - core}, device_id_type=MESH,
    ).start()
    wait_all(pair, 4)
    chip = c * ny + y
    chips[chip] = pair[0] + pair[1]
    for dz, dx in order:
        for dy in range(ny - 1, -1, -1):
            if dz or dx or dy:
                to_row = 2 * lax.rem(y + dy, ny) + core
                to_col = lax.rem(z + dz, nz) * NX + lax.rem(x + dx, NX)
                pltpu.make_async_remote_copy(
                    src_ref=chips.at[chip], dst_ref=chips.at[chip],
                    send_sem=ssem.at[5], recv_sem=rsem.at[5],
                    device_id={"row": to_row, "col": to_col}, device_id_type=MESH,
                ).start()

    wait_all(ag_recv, 3)
    r_o[...] = ag_recv[...].reshape(n_col, LANES)
    col_rsqrt = lax.rsqrt(turned_col)

    def raw_chunk(i):
        size = min(LANES, local_rows - i * LANES)
        factor = lax.rsqrt(ag_recv[i // nz, pl.ds(i % nz, 1), :])
        raw_o[pl.ds(i * LANES, size), :] = (grad[i] * factor * col_rsqrt).T[:size]

    for i in range(pl.cdiv(local_rows, LANES)):
        raw_chunk(i)
    wait_all(chips, 5)
    totals = jnp.sum(chips[...], axis=0)

    def pick_lane(k):
        return jnp.broadcast_to(
            jnp.sum(jnp.where(lane == k, totals, 0.0), axis=1, keepdims=True), (1, LANES)
        )

    mean_row = pick_lane(0) / float(total_rows)
    clip = jnp.maximum(1.0, jnp.sqrt(mean_row * pick_lane(1) / cells))
    root = jnp.sqrt(mean_row)
    step = RATE * jnp.sqrt(pick_lane(2) / cells)
    scal_o[0:1, :] = root / clip
    scal_o[1:2, :] = step
    scal_o[2:3, :] = root
    scal_o[3:8, :] = jnp.zeros((5, LANES), F32)

    sent_all(recv, a2a_ssem)
    for q, buf in enumerate((col_recv, rs_recv, q_recv, ag_recv, pair, chips)):
        sent_all(buf, ssem.at[q])


def write_kernel(
    local_rows, raw, pv, rows, new_col, scal,
    np_o, up_o, nr_o, nc_o, rf_o,
    npv, upv, nrv, ncv, rfv, out_sem, small_sem,
):
    count = 10
    size = local_rows // count
    k = scal[0:1, :]
    step = scal[1:2, :]
    root = scal[2:3, :]
    small = []
    for i in range(count):
        span = pl.ds(i * size, size)
        update = raw[span, :] * k
        upv[span, :] = update
        pltpu.make_async_copy(upv.at[span], up_o.at[span], out_sem.at[0]).start()
        npv[span, :] = pv[span, :] - step * update
        pltpu.make_async_copy(npv.at[span], np_o.at[span], out_sem.at[1]).start()
        if i == 0:
            values = rows[...]
            factor = lax.rsqrt(values) * root
            for j in range(pl.cdiv(local_rows, LANES)):
                n = min(LANES, local_rows - j * LANES)
                nrv[pl.ds(j * LANES, n)] = values[j, :n]
                rfv[pl.ds(j * LANES, n)] = factor[j, :n]
            ncv[...] = new_col[0, :]
            for q, (src, dst) in enumerate(((nrv, nr_o), (rfv, rf_o), (ncv, nc_o))):
                small.append(pltpu.make_async_copy(src, dst, small_sem.at[q]))
                small[-1].start()
    pltpu.make_async_copy(upv, up_o, out_sem.at[0]).wait()
    pltpu.make_async_copy(npv, np_o, out_sem.at[1]).wait()
    for copy in small:
        copy.wait()


def body(n_row, n_col, cotangent, token_ids, param, row_moment, col_moment):
    local_rows, width = param.shape
    total_rows = local_rows * n_row
    total_cols = width * n_col
    nz = n_col // NX
    vmem = pl.BlockSpec(memory_space=pltpu.VMEM)
    hbm = pl.BlockSpec(memory_space=pltpu.HBM)
    dma = pltpu.SemaphoreType.DMA

    ids_shape = (n_col * BLOCK // LANES, LANES)

    def stay(value):
        return pltpu.with_memory_space_constraint(value, pltpu.HBM)

    raw, pv, rows, new_col, scal = pl.pallas_call(
        functools.partial(step_kernel, n_row, n_col, local_rows, total_rows, total_cols),
        out_shape=(
            pltpu.VMEM((local_rows, LANES), F32),
            pltpu.VMEM((local_rows, LANES), F32),
            pltpu.VMEM((n_col, LANES), F32),
            pltpu.VMEM((1, LANES), F32),
            pltpu.VMEM((8, LANES), F32),
        ),
        in_specs=[hbm] * 5,
        out_specs=(vmem,) * 5,
        scratch_shapes=[
            pltpu.VMEM((nz, BLOCK, NX * LANES), BF16),
            pltpu.VMEM(ids_shape, jnp.int32),
            pltpu.VMEM((local_rows,), F32),
            pltpu.VMEM((n_col, LANES), F32),
            pltpu.VMEM((1, LANES), F32),
            pltpu.VMEM(ids_shape, F32),
            pltpu.VMEM(ids_shape, F32),
            pltpu.VMEM(ids_shape, F32),
            pltpu.VMEM((n_col, CAP, LANES), BF16),
            pltpu.VMEM((n_col, CAP, LANES), BF16),
            pltpu.VMEM((2, n_col // 2, GROUP * CAP, 2 * LANES), BF16),
            pltpu.VMEM((nz, NX, CAP, LANES), BF16),
            pltpu.VMEM((n_col, CAP, LANES), BF16),
            pltpu.VMEM((n_col, LANES, LANES), F32),
            pltpu.VMEM((1, 1, LANES), F32),
            pltpu.VMEM((n_row, 1, LANES), F32),
            pltpu.VMEM((NX, nz, LANES), F32),
            pltpu.VMEM((n_col, nz, LANES), F32),
            pltpu.VMEM((NX, nz, LANES), F32),
            pltpu.VMEM((NX, nz, LANES), F32),
            pltpu.VMEM((NX, nz, LANES), F32),
            pltpu.VMEM((2, 1, LANES), F32),
            pltpu.VMEM((n_col * n_row // 2, 1, LANES), F32),
            dma((4,)),
            dma,
            dma,
            dma((n_col // GROUP,)),
            dma((6,)),
            dma((6,)),
        ],
        compiler_params=pltpu.CompilerParams(
            collective_id=0, has_side_effects=True, vmem_limit_bytes=32 * 1024 * 1024
        ),
        name="adafactor_step",
    )(
        stay(cotangent), stay(token_ids.reshape(ids_shape)), stay(param), stay(row_moment),
        stay(col_moment.reshape(1, LANES)),
    )

    return pl.pallas_call(
        functools.partial(write_kernel, local_rows),
        out_shape=(
            jax.ShapeDtypeStruct((local_rows, LANES), F32),
            jax.ShapeDtypeStruct((local_rows, LANES), F32),
            jax.ShapeDtypeStruct((local_rows,), F32),
            jax.ShapeDtypeStruct((LANES,), F32),
            jax.ShapeDtypeStruct((local_rows,), F32),
        ),
        in_specs=[vmem] * 5,
        out_specs=(hbm,) * 5,
        scratch_shapes=[
            pltpu.VMEM((local_rows, LANES), F32),
            pltpu.VMEM((local_rows, LANES), F32),
            pltpu.VMEM((local_rows,), F32),
            pltpu.VMEM((LANES,), F32),
            pltpu.VMEM((local_rows,), F32),
            dma((2,)),
            dma((3,)),
        ],
        compiler_params=pltpu.CompilerParams(vmem_limit_bytes=16 * 1024 * 1024),
        name="adafactor_write",
    )(raw, pv, rows, new_col, scal)


def solution(mesh):
    n_row, n_col = mesh.shape["row"], mesh.shape["col"]
    in_specs = (P("col", None), P(), P("row", "col"), P("row"), P("col"))
    out_specs = (P("row", "col"), P("row", "col"), P("row"), P("col"), P("row"))
    return jax.shard_map(
        functools.partial(body, n_row, n_col),
        mesh=mesh, in_specs=in_specs, out_specs=out_specs, check_vma=False,
    )
```

```python
import functools

import jax
import jax.numpy as jnp
from jax import lax
from jax.experimental import pallas as pl
from jax.experimental.pallas import tpu as pltpu
from jax.sharding import PartitionSpec as P

STEP = 100
DECAY = 1.0 - STEP ** (-0.8)
RATE = min(0.01, STEP ** (-0.5))
TINY = 1e-30
CAP = 64
BLOCK = 256
LANES = 128
NX = 4
GROUP = 4
MESH = pl.DeviceIdType.MESH
F32 = jnp.float32
BF16 = jnp.bfloat16


def iota(shape, dim):
    return lax.broadcasted_iota(jnp.int32, shape, dim)


def dot(a, b):
    return jnp.dot(a, b, preferred_element_type=F32)


def dot_nt(a, b):
    return lax.dot_general(a, b, (((1,), (1,)), ((), ())), preferred_element_type=F32)


def order_of(nz):
    far = sorted(range(nz), key=lambda d: (-min(d, nz - d), d))
    return [(dz, dx) for dx in (2, 1, 3, 0) for dz in far]


def step_kernel(
    n_row, n_col, local_rows, total_rows, total_cols,
    cot, ids_hbm, param, rowm_hbm, colm_hbm,
    raw_o, pv_o, r_o, nc_o, scal_o,
    cotv, ids, rowm, moments, colm, posv, hiv, lov, high, low, ready, send, recv, grad,
    col_send, col_recv, rs_send, rs_recv, q_send, q_recv,
    ag_recv, pair, chips,
    in_sem, cot_sem, a2a_ssem, a2a_rsem, ssem, rsem,
):
    nz = n_col // NX
    cells = float(total_rows) * float(total_cols)
    width = NX * LANES
    r = lax.axis_index("row")
    c = lax.axis_index("col")
    z = c // NX
    x = lax.rem(c, NX)
    y = r // 2
    core = lax.rem(r, 2)
    ny = n_row // 2
    order = order_of(nz)

    barrier = pltpu.get_barrier_semaphore()
    for dz, dx in order[:-1]:
        peer = lax.rem(z + dz, nz) * NX + lax.rem(x + dx, NX)
        pl.semaphore_signal(barrier, inc=1, device_id={"col": peer}, device_id_type=MESH)
    for k in range(1, n_row):
        pl.semaphore_signal(
            barrier, inc=1, device_id={"row": lax.rem(r + k, n_row)}, device_id_type=MESH
        )

    ids_copy = pltpu.make_async_copy(ids_hbm, ids, in_sem.at[0])
    ids_copy.start()

    def cot_copy(j):
        zt = lax.rem(z + j, nz)
        return pltpu.make_async_copy(
            cot.at[:, pl.ds(pl.multiple_of(zt * width, width), width)], cotv.at[j], cot_sem
        )

    for j in range(nz):
        cot_copy(j).start()

    rowm_copy = pltpu.make_async_copy(rowm_hbm, rowm, in_sem.at[1])
    rowm_copy.start()
    colm_copy = pltpu.make_async_copy(colm_hbm, colm, in_sem.at[2])
    colm_copy.start()
    param_copy = pltpu.make_async_copy(param, pv_o, in_sem.at[3])
    param_copy.start()

    ids_copy.wait()
    local = ids[...] - r * local_rows
    inside = (local >= 0) & (local < local_rows)
    ones = jnp.where(inside, 1.0, 0.0).astype(BF16)
    before = jnp.where(iota((LANES, LANES), 0) < iota((LANES, LANES), 1), 1.0, 0.0).astype(BF16)
    count = dot(ones, before)
    total = dot(ones, jnp.ones((LANES, LANES), BF16))
    odd = lax.rem(iota(local.shape, 0), 2) == 1
    position = count + jnp.where(odd, pltpu.roll(total, 1, 0), 0.0)
    posv[...] = jnp.where(inside, position, -1000.0)
    hiv[...] = jnp.where(inside, (local >> 7) + 1, 0).astype(F32)
    lov[...] = jnp.where(inside, local & 127, 0).astype(F32)

    slot_iota = iota((CAP, LANES), 0).astype(F32)

    def picks(block):
        return jnp.concatenate(
            [
                jnp.where(posv[pl.ds(2 * block + h, 1), :] == slot_iota, 1.0, 0.0).astype(BF16)
                for h in range(2)
            ],
            axis=1,
        )

    pick = picks(c)

    pltpu.make_async_copy(cotv, cotv, cot_sem).wait()
    for j in range(nz):
        packed = dot(pick, cotv[j]).astype(BF16)
        for k in range(NX):
            send[j, k] = packed[:, k * LANES:(k + 1) * LANES]
    recv[c] = send[0, x]
    pl.semaphore_wait(barrier, n_col + n_row - 2)
    for n, (dz, dx) in enumerate(order[:-1]):
        xt = lax.rem(x + dx, NX)
        pltpu.make_async_remote_copy(
            src_ref=send.at[dz, xt], dst_ref=recv.at[c],
            send_sem=a2a_ssem, recv_sem=a2a_rsem.at[n // GROUP],
            device_id={"col": lax.rem(z + dz, nz) * NX + xt}, device_id_type=MESH,
        ).start()

    lane_iota = iota((CAP, LANES), 1).astype(F32)

    def slot_step(b, carry):
        found = jnp.zeros((CAP, 2 * LANES), F32)
        both = picks(b)
        for h in range(2):
            row = pl.ds(2 * b + h, 1)
            values = jnp.concatenate(
                [
                    jnp.broadcast_to(hiv[row, :], (LANES, LANES)),
                    jnp.broadcast_to(lov[row, :], (LANES, LANES)),
                ],
                axis=0,
            ).astype(BF16)
            found = found + dot_nt(both[:, h * LANES:(h + 1) * LANES], values)
        high[b] = found[:, :LANES].astype(BF16)
        low[b] = jnp.where(found[:, LANES:] == lane_iota, 1.0, 0.0).astype(BF16)
        return carry

    lax.fori_loop(0, n_col, slot_step, 0, unroll=8)

    param_copy.wait()
    ptile = local_rows // 5

    def param_step(i, acc):
        block = pv_o[pl.ds(pl.multiple_of(i * ptile, 8), ptile), :]
        return acc + jnp.sum((block * block).reshape(ptile // 8, 8, LANES), axis=0)

    acc = lax.fori_loop(0, 5, param_step, jnp.zeros((8, LANES), F32))
    param_local = jnp.sum(jnp.sum(acc, axis=0, keepdims=True), axis=1, keepdims=True)

    grad[...] = jnp.zeros_like(grad)


    last = n_col // GROUP - 1
    kept = range(max(0, last - 1), last + 1)

    def sources(j):
        return [
            lax.rem(z + nz - dz, nz) * NX + lax.rem(x + NX - dx, NX)
            for dz, dx in order[j * GROUP:(j + 1) * GROUP]
        ]

    def onehots(j):
        hi = jnp.concatenate([high[src] for src in sources(j)], axis=0)
        lo = jnp.concatenate([low[src] for src in sources(j)], axis=0)
        zero = jnp.zeros_like(lo)
        for i in range(n_col // 2):
            yield jnp.concatenate(
                [jnp.where(hi == jnp.asarray(2 * i + h + 1, BF16), lo, zero) for h in range(2)], axis=1
            )

    for j in kept:
        for i, onehot in enumerate(onehots(j)):
            ready[j - kept[0], i] = onehot

    def parts(j):
        arrivals = sum(1 for member in order[j * GROUP:(j + 1) * GROUP] if member != (0, 0))
        landed = recv.at[pl.ds(0, arrivals)]
        pltpu.make_async_copy(landed, landed, a2a_rsem.at[j]).wait()
        turned = jnp.concatenate([recv[src] for src in sources(j)], axis=0).T
        made = (ready[j - kept[0], i] for i in range(n_col // 2)) if j in kept else onehots(j)
        for i, onehot in enumerate(made):
            part = dot(turned, onehot)
            for h in range(2):
                yield 2 * i + h, part[:, h * LANES:(h + 1) * LANES]

    for j in range(last):
        for i, part in parts(j):
            grad[i] += part
    acc = jnp.zeros((LANES, LANES), F32)
    for i, part in parts(last):
        value = grad[i] + part
        grad[i] = value
        acc = acc + value * value

    def exchange(src, dst, me, axis, q):
        for k in range(1, {"row": n_row, "x": NX, "col": n_col}[axis]):
            if axis == "row":
                device = {"row": lax.rem(r + k, n_row)}
                quarter = 0
            elif axis == "x":
                quarter = lax.rem(x + k, NX)
                device = {"col": z * NX + quarter}
            else:
                dz, dx = order[k - 1]
                quarter = lax.rem(x + dx, NX)
                device = {"col": lax.rem(z + dz, nz) * NX + quarter}
            pltpu.make_async_remote_copy(
                src_ref=src.at[quarter if src.shape[0] > 1 else 0], dst_ref=dst.at[me],
                send_sem=ssem.at[q], recv_sem=rsem.at[q],
                device_id=device, device_id_type=MESH,
            ).start()

    def wait_all(buf, q):
        rest = buf.at[pl.ds(0, buf.shape[0] - 1)]
        pltpu.make_async_copy(rest, rest, rsem.at[q]).wait()

    def sent_all(buf, sem):
        rest = buf.at[pl.ds(0, buf.shape[0] - 1)]
        pltpu.make_async_remote_copy(
            src_ref=rest, dst_ref=rest, send_sem=sem, recv_sem=sem,
            device_id={"row": lax.rem(r + 1, n_row)}, device_id_type=MESH,
        ).wait_send()

    col_send[0] = jnp.sum(acc.T, axis=0, keepdims=True)
    exchange(col_send, col_recv, r, "row", 0)
    for i in range(n_col):
        value = grad[i]
        rs_send[i // nz, pl.ds(i % nz, 1), :] = jnp.sum(value * value, axis=0, keepdims=True)
    exchange(rs_send, rs_recv, c, "col", 1)
    rs_recv[c] = rs_send[x]
    col_recv[r] = col_send[0]
    colm_copy.wait()
    rowm_copy.wait()
    for i in range(n_col):
        size = max(0, min(LANES, local_rows - i * LANES))
        if size < LANES:
            moments[pl.ds(i, 1), :] = jnp.ones((1, LANES), F32)
        if size:
            moments[i, :size] = rowm[pl.ds(i * LANES, size)]

    wait_all(col_recv, 0)
    col_total = jnp.sum(col_recv[...], axis=0)
    new_col = DECAY * colm[...] + (1.0 - DECAY) * (col_total / float(total_rows) + TINY)
    nc_o[...] = new_col
    turned_col = jnp.broadcast_to(new_col, (LANES, LANES)).T
    inverse_col = 1.0 / turned_col
    for i in range(n_col):
        value = grad[i]
        q_send[i // nz, pl.ds(i % nz, 1), :] = jnp.sum(value * value * inverse_col, axis=0, keepdims=True)
    exchange(q_send, q_recv, x, "x", 2)
    q_recv[x] = q_send[x]

    wait_all(rs_recv, 1)
    row_total = jnp.sum(rs_recv[...], axis=0)
    moment = moments[pl.ds(pl.multiple_of(x * nz, nz), nz), :]
    new_row = DECAY * moment + (1.0 - DECAY) * (row_total / float(total_cols) + TINY)
    ag_recv[x] = new_row
    exchange(ag_recv.at[pl.ds(x, 1)], ag_recv, x, "x", 3)
    wait_all(q_recv, 2)
    row_id = x * (nz * LANES) + iota((nz, LANES), 0) * LANES + iota((nz, LANES), 1)
    valid = row_id < local_rows
    raw_part = jnp.sum(q_recv[...], axis=0) / new_row

    def total_of(value):
        return jnp.sum(jnp.sum(jnp.where(valid, value, 0.0), axis=0, keepdims=True), axis=1, keepdims=True)

    lane = iota((1, LANES), 1)
    row_sum = total_of(new_row) * (1.0 / nz)
    raw_sum = total_of(raw_part)
    pair[core] = jnp.where(
        lane == 0, row_sum, jnp.where(lane == 1, raw_sum, jnp.where(lane == 2, param_local, 0.0))
    )
    pltpu.make_async_remote_copy(
        src_ref=pair.at[core], dst_ref=pair.at[core], send_sem=ssem.at[4], recv_sem=rsem.at[4],
        device_id={"row": 2 * y + 1 - core}, device_id_type=MESH,
    ).start()
    wait_all(pair, 4)
    chip = c * ny + y
    chips[chip] = pair[0] + pair[1]
    for dz, dx in order:
        for dy in range(ny - 1, -1, -1):
            if dz or dx or dy:
                to_row = 2 * lax.rem(y + dy, ny) + core
                to_col = lax.rem(z + dz, nz) * NX + lax.rem(x + dx, NX)
                pltpu.make_async_remote_copy(
                    src_ref=chips.at[chip], dst_ref=chips.at[chip],
                    send_sem=ssem.at[5], recv_sem=rsem.at[5],
                    device_id={"row": to_row, "col": to_col}, device_id_type=MESH,
                ).start()

    wait_all(ag_recv, 3)
    r_o[...] = ag_recv[...].reshape(n_col, LANES)
    col_rsqrt = lax.rsqrt(turned_col)

    def raw_chunk(i):
        size = min(LANES, local_rows - i * LANES)
        factor = lax.rsqrt(ag_recv[i // nz, pl.ds(i % nz, 1), :])
        raw_o[pl.ds(i * LANES, size), :] = (grad[i] * factor * col_rsqrt).T[:size]

    for i in range(pl.cdiv(local_rows, LANES)):
        raw_chunk(i)
    wait_all(chips, 5)
    totals = jnp.sum(chips[...], axis=0)

    def pick_lane(k):
        return jnp.broadcast_to(
            jnp.sum(jnp.where(lane == k, totals, 0.0), axis=1, keepdims=True), (1, LANES)
        )

    mean_row = pick_lane(0) / float(total_rows)
    clip = jnp.maximum(1.0, jnp.sqrt(mean_row * pick_lane(1) / cells))
    root = jnp.sqrt(mean_row)
    step = RATE * jnp.sqrt(pick_lane(2) / cells)
    scal_o[0:1, :] = root / clip
    scal_o[1:2, :] = step
    scal_o[2:3, :] = root
    scal_o[3:8, :] = jnp.zeros((5, LANES), F32)

    sent_all(recv, a2a_ssem)
    for q, buf in enumerate((col_recv, rs_recv, q_recv, ag_recv, pair, chips)):
        sent_all(buf, ssem.at[q])


def write_kernel(
    local_rows, raw, pv, rows, new_col, scal,
    np_o, up_o, nr_o, nc_o, rf_o,
    npv, upv, nrv, ncv, rfv, out_sem, small_sem,
):
    count = 10
    size = local_rows // count
    k = scal[0:1, :]
    step = scal[1:2, :]
    root = scal[2:3, :]
    small = []
    for i in range(count):
        span = pl.ds(i * size, size)
        update = raw[span, :] * k
        upv[span, :] = update
        pltpu.make_async_copy(upv.at[span], up_o.at[span], out_sem.at[0]).start()
        npv[span, :] = pv[span, :] - step * update
        pltpu.make_async_copy(npv.at[span], np_o.at[span], out_sem.at[1]).start()
        if i == 0:
            values = rows[...]
            factor = lax.rsqrt(values) * root
            for j in range(pl.cdiv(local_rows, LANES)):
                n = min(LANES, local_rows - j * LANES)
                nrv[pl.ds(j * LANES, n)] = values[j, :n]
                rfv[pl.ds(j * LANES, n)] = factor[j, :n]
            ncv[...] = new_col[0, :]
            for q, (src, dst) in enumerate(((nrv, nr_o), (rfv, rf_o), (ncv, nc_o))):
                small.append(pltpu.make_async_copy(src, dst, small_sem.at[q]))
                small[-1].start()
    pltpu.make_async_copy(upv, up_o, out_sem.at[0]).wait()
    pltpu.make_async_copy(npv, np_o, out_sem.at[1]).wait()
    for copy in small:
        copy.wait()


def body(n_row, n_col, cotangent, token_ids, param, row_moment, col_moment):
    local_rows, width = param.shape
    total_rows = local_rows * n_row
    total_cols = width * n_col
    nz = n_col // NX
    vmem = pl.BlockSpec(memory_space=pltpu.VMEM)
    hbm = pl.BlockSpec(memory_space=pltpu.HBM)
    dma = pltpu.SemaphoreType.DMA

    ids_shape = (n_col * BLOCK // LANES, LANES)

    def stay(value):
        return pltpu.with_memory_space_constraint(value, pltpu.HBM)

    raw, pv, rows, new_col, scal = pl.pallas_call(
        functools.partial(step_kernel, n_row, n_col, local_rows, total_rows, total_cols),
        out_shape=(
            pltpu.VMEM((local_rows, LANES), F32),
            pltpu.VMEM((local_rows, LANES), F32),
            pltpu.VMEM((n_col, LANES), F32),
            pltpu.VMEM((1, LANES), F32),
            pltpu.VMEM((8, LANES), F32),
        ),
        in_specs=[hbm] * 5,
        out_specs=(vmem,) * 5,
        scratch_shapes=[
            pltpu.VMEM((nz, BLOCK, NX * LANES), BF16),
            pltpu.VMEM(ids_shape, jnp.int32),
            pltpu.VMEM((local_rows,), F32),
            pltpu.VMEM((n_col, LANES), F32),
            pltpu.VMEM((1, LANES), F32),
            pltpu.VMEM(ids_shape, F32),
            pltpu.VMEM(ids_shape, F32),
            pltpu.VMEM(ids_shape, F32),
            pltpu.VMEM((n_col, CAP, LANES), BF16),
            pltpu.VMEM((n_col, CAP, LANES), BF16),
            pltpu.VMEM((2, n_col // 2, GROUP * CAP, 2 * LANES), BF16),
            pltpu.VMEM((nz, NX, CAP, LANES), BF16),
            pltpu.VMEM((n_col, CAP, LANES), BF16),
            pltpu.VMEM((n_col, LANES, LANES), F32),
            pltpu.VMEM((1, 1, LANES), F32),
            pltpu.VMEM((n_row, 1, LANES), F32),
            pltpu.VMEM((NX, nz, LANES), F32),
            pltpu.VMEM((n_col, nz, LANES), F32),
            pltpu.VMEM((NX, nz, LANES), F32),
            pltpu.VMEM((NX, nz, LANES), F32),
            pltpu.VMEM((NX, nz, LANES), F32),
            pltpu.VMEM((2, 1, LANES), F32),
            pltpu.VMEM((n_col * n_row // 2, 1, LANES), F32),
            dma((4,)),
            dma,
            dma,
            dma((n_col // GROUP,)),
            dma((6,)),
            dma((6,)),
        ],
        compiler_params=pltpu.CompilerParams(
            collective_id=0, has_side_effects=True, vmem_limit_bytes=32 * 1024 * 1024
        ),
        name="adafactor_step",
    )(
        stay(cotangent), stay(token_ids.reshape(ids_shape)), stay(param), stay(row_moment),
        stay(col_moment.reshape(1, LANES)),
    )

    return pl.pallas_call(
        functools.partial(write_kernel, local_rows),
        out_shape=(
            jax.ShapeDtypeStruct((local_rows, LANES), F32),
            jax.ShapeDtypeStruct((local_rows, LANES), F32),
            jax.ShapeDtypeStruct((local_rows,), F32),
            jax.ShapeDtypeStruct((LANES,), F32),
            jax.ShapeDtypeStruct((local_rows,), F32),
        ),
        in_specs=[vmem] * 5,
        out_specs=(hbm,) * 5,
        scratch_shapes=[
            pltpu.VMEM((local_rows, LANES), F32),
            pltpu.VMEM((local_rows, LANES), F32),
            pltpu.VMEM((local_rows,), F32),
            pltpu.VMEM((LANES,), F32),
            pltpu.VMEM((local_rows,), F32),
            dma((2,)),
            dma((3,)),
        ],
        compiler_params=pltpu.CompilerParams(vmem_limit_bytes=16 * 1024 * 1024),
        name="adafactor_write",
    )(raw, pv, rows, new_col, scal)


def solution(mesh):
    n_row, n_col = mesh.shape["row"], mesh.shape["col"]
    in_specs = (P("col", None), P(), P("row", "col"), P("row"), P("col"))
    out_specs = (P("row", "col"), P("row", "col"), P("row"), P("col"), P("row"))
    return jax.shard_map(
        functools.partial(body, n_row, n_col),
        mesh=mesh, in_specs=in_specs, out_specs=out_specs, check_vma=False,
    )
```

```python
import functools

import jax
import jax.numpy as jnp
from jax import lax
from jax.experimental import pallas as pl
from jax.experimental.pallas import tpu as pltpu
from jax.sharding import PartitionSpec as P

STEP = 100
DECAY = 1.0 - STEP ** (-0.8)
RATE = min(0.01, STEP ** (-0.5))
TINY = 1e-30
CAP = 64
BLOCK = 256
LANES = 128
NX = 4
GROUP = 4
MESH = pl.DeviceIdType.MESH
F32 = jnp.float32
BF16 = jnp.bfloat16


def iota(shape, dim):
    return lax.broadcasted_iota(jnp.int32, shape, dim)


def dot(a, b):
    return jnp.dot(a, b, preferred_element_type=F32)


def dot_nt(a, b):
    return lax.dot_general(a, b, (((1,), (1,)), ((), ())), preferred_element_type=F32)


def order_of(nz):
    far = sorted(range(nz), key=lambda d: (-min(d, nz - d), d))
    sides = [(dz, dx) for dz in far for dx in (1, 3)]
    return [(dz, 2) for dz in far] + sides + [(dz, 0) for dz in far]


def step_kernel(
    n_row, n_col, local_rows, total_rows, total_cols,
    cot, ids_hbm, param, rowm_hbm, colm_hbm,
    raw_o, pv_o, r_o, nc_o, scal_o,
    cotv, ids, rowm, moments, colm, posv, hiv, lov, high, low, ready, send, recv, grad,
    col_send, col_recv, rs_send, rs_recv, q_send, q_recv,
    ag_recv, pair, chips,
    in_sem, cot_sem, a2a_ssem, a2a_rsem, ssem, rsem,
):
    nz = n_col // NX
    cells = float(total_rows) * float(total_cols)
    width = NX * LANES
    r = lax.axis_index("row")
    c = lax.axis_index("col")
    z = c // NX
    x = lax.rem(c, NX)
    y = r // 2
    core = lax.rem(r, 2)
    ny = n_row // 2
    order = order_of(nz)

    barrier = pltpu.get_barrier_semaphore()
    for dz, dx in order[:-1]:
        peer = lax.rem(z + dz, nz) * NX + lax.rem(x + dx, NX)
        pl.semaphore_signal(barrier, inc=1, device_id={"col": peer}, device_id_type=MESH)
    for k in range(1, n_row):
        pl.semaphore_signal(
            barrier, inc=1, device_id={"row": lax.rem(r + k, n_row)}, device_id_type=MESH
        )

    ids_copy = pltpu.make_async_copy(ids_hbm, ids, in_sem.at[0])
    ids_copy.start()

    def cot_copy(j):
        zt = lax.rem(z + j, nz)
        return pltpu.make_async_copy(
            cot.at[:, pl.ds(pl.multiple_of(zt * width, width), width)], cotv.at[j], cot_sem
        )

    for j in range(nz):
        cot_copy(j).start()

    rowm_copy = pltpu.make_async_copy(rowm_hbm, rowm, in_sem.at[1])
    rowm_copy.start()
    colm_copy = pltpu.make_async_copy(colm_hbm, colm, in_sem.at[2])
    colm_copy.start()
    param_copy = pltpu.make_async_copy(param, pv_o, in_sem.at[3])
    param_copy.start()

    ids_copy.wait()
    local = ids[...] - r * local_rows
    inside = (local >= 0) & (local < local_rows)
    ones = jnp.where(inside, 1.0, 0.0).astype(BF16)
    before = jnp.where(iota((LANES, LANES), 0) < iota((LANES, LANES), 1), 1.0, 0.0).astype(BF16)
    count = dot(ones, before)
    total = dot(ones, jnp.ones((LANES, LANES), BF16))
    odd = lax.rem(iota(local.shape, 0), 2) == 1
    position = count + jnp.where(odd, pltpu.roll(total, 1, 0), 0.0)
    posv[...] = jnp.where(inside, position, -1000.0)
    hiv[...] = jnp.where(inside, (local >> 7) + 1, 0).astype(F32)
    lov[...] = jnp.where(inside, local & 127, 0).astype(F32)

    slot_iota = iota((CAP, LANES), 0).astype(F32)

    def picks(block):
        return jnp.concatenate(
            [
                jnp.where(posv[pl.ds(2 * block + h, 1), :] == slot_iota, 1.0, 0.0).astype(BF16)
                for h in range(2)
            ],
            axis=1,
        )

    pick = picks(c)

    pltpu.make_async_copy(cotv, cotv, cot_sem).wait()
    for j in range(nz):
        packed = dot(pick, cotv[j]).astype(BF16)
        for k in range(NX):
            send[j, k] = packed[:, k * LANES:(k + 1) * LANES]
    recv[c] = send[0, x]
    pl.semaphore_wait(barrier, n_col + n_row - 2)
    for n, (dz, dx) in enumerate(order[:-1]):
        xt = lax.rem(x + dx, NX)
        pltpu.make_async_remote_copy(
            src_ref=send.at[dz, xt], dst_ref=recv.at[c],
            send_sem=a2a_ssem, recv_sem=a2a_rsem.at[n // GROUP],
            device_id={"col": lax.rem(z + dz, nz) * NX + xt}, device_id_type=MESH,
        ).start()

    lane_iota = iota((CAP, LANES), 1).astype(F32)

    def slot_step(b, carry):
        found = jnp.zeros((CAP, 2 * LANES), F32)
        both = picks(b)
        for h in range(2):
            row = pl.ds(2 * b + h, 1)
            values = jnp.concatenate(
                [
                    jnp.broadcast_to(hiv[row, :], (LANES, LANES)),
                    jnp.broadcast_to(lov[row, :], (LANES, LANES)),
                ],
                axis=0,
            ).astype(BF16)
            found = found + dot_nt(both[:, h * LANES:(h + 1) * LANES], values)
        high[b] = found[:, :LANES].astype(BF16)
        low[b] = jnp.where(found[:, LANES:] == lane_iota, 1.0, 0.0).astype(BF16)
        return carry

    lax.fori_loop(0, n_col, slot_step, 0, unroll=8)

    param_copy.wait()
    ptile = local_rows // 5

    def param_step(i, acc):
        block = pv_o[pl.ds(pl.multiple_of(i * ptile, 8), ptile), :]
        return acc + jnp.sum((block * block).reshape(ptile // 8, 8, LANES), axis=0)

    acc = lax.fori_loop(0, 5, param_step, jnp.zeros((8, LANES), F32))
    param_local = jnp.sum(jnp.sum(acc, axis=0, keepdims=True), axis=1, keepdims=True)

    grad[...] = jnp.zeros_like(grad)


    last = n_col // GROUP - 1
    kept = range(max(0, last - 1), last + 1)

    def sources(j):
        return [
            lax.rem(z + nz - dz, nz) * NX + lax.rem(x + NX - dx, NX)
            for dz, dx in order[j * GROUP:(j + 1) * GROUP]
        ]

    def onehots(j):
        hi = jnp.concatenate([high[src] for src in sources(j)], axis=0)
        lo = jnp.concatenate([low[src] for src in sources(j)], axis=0)
        zero = jnp.zeros_like(lo)
        for i in range(n_col // 2):
            yield jnp.concatenate(
                [jnp.where(hi == jnp.asarray(2 * i + h + 1, BF16), lo, zero) for h in range(2)], axis=1
            )

    for j in kept:
        for i, onehot in enumerate(onehots(j)):
            ready[j - kept[0], i] = onehot

    def parts(j):
        arrivals = sum(1 for member in order[j * GROUP:(j + 1) * GROUP] if member != (0, 0))
        landed = recv.at[pl.ds(0, arrivals)]
        pltpu.make_async_copy(landed, landed, a2a_rsem.at[j]).wait()
        turned = jnp.concatenate([recv[src] for src in sources(j)], axis=0).T
        made = (ready[j - kept[0], i] for i in range(n_col // 2)) if j in kept else onehots(j)
        for i, onehot in enumerate(made):
            part = dot(turned, onehot)
            for h in range(2):
                yield 2 * i + h, part[:, h * LANES:(h + 1) * LANES]

    for j in range(last):
        for i, part in parts(j):
            grad[i] += part
    acc = jnp.zeros((LANES, LANES), F32)
    for i, part in parts(last):
        value = grad[i] + part
        grad[i] = value
        acc = acc + value * value

    def exchange(src, dst, me, axis, q):
        for k in range(1, {"row": n_row, "x": NX, "col": n_col}[axis]):
            if axis == "row":
                device = {"row": lax.rem(r + k, n_row)}
                quarter = 0
            elif axis == "x":
                quarter = lax.rem(x + k, NX)
                device = {"col": z * NX + quarter}
            else:
                dz, dx = order[k - 1]
                quarter = lax.rem(x + dx, NX)
                device = {"col": lax.rem(z + dz, nz) * NX + quarter}
            pltpu.make_async_remote_copy(
                src_ref=src.at[quarter if src.shape[0] > 1 else 0], dst_ref=dst.at[me],
                send_sem=ssem.at[q], recv_sem=rsem.at[q],
                device_id=device, device_id_type=MESH,
            ).start()

    def wait_all(buf, q):
        rest = buf.at[pl.ds(0, buf.shape[0] - 1)]
        pltpu.make_async_copy(rest, rest, rsem.at[q]).wait()

    def sent_all(buf, sem):
        rest = buf.at[pl.ds(0, buf.shape[0] - 1)]
        pltpu.make_async_remote_copy(
            src_ref=rest, dst_ref=rest, send_sem=sem, recv_sem=sem,
            device_id={"row": lax.rem(r + 1, n_row)}, device_id_type=MESH,
        ).wait_send()

    col_send[0] = jnp.sum(acc.T, axis=0, keepdims=True)
    exchange(col_send, col_recv, r, "row", 0)
    for i in range(n_col):
        value = grad[i]
        rs_send[i // nz, pl.ds(i % nz, 1), :] = jnp.sum(value * value, axis=0, keepdims=True)
    exchange(rs_send, rs_recv, c, "col", 1)
    rs_recv[c] = rs_send[x]
    col_recv[r] = col_send[0]
    colm_copy.wait()
    rowm_copy.wait()
    for i in range(n_col):
        size = max(0, min(LANES, local_rows - i * LANES))
        if size < LANES:
            moments[pl.ds(i, 1), :] = jnp.ones((1, LANES), F32)
        if size:
            moments[i, :size] = rowm[pl.ds(i * LANES, size)]

    wait_all(col_recv, 0)
    col_total = jnp.sum(col_recv[...], axis=0)
    new_col = DECAY * colm[...] + (1.0 - DECAY) * (col_total / float(total_rows) + TINY)
    nc_o[...] = new_col
    turned_col = jnp.broadcast_to(new_col, (LANES, LANES)).T
    inverse_col = 1.0 / turned_col
    for i in range(n_col):
        value = grad[i]
        q_send[i // nz, pl.ds(i % nz, 1), :] = jnp.sum(value * value * inverse_col, axis=0, keepdims=True)
    exchange(q_send, q_recv, x, "x", 2)
    q_recv[x] = q_send[x]

    wait_all(rs_recv, 1)
    row_total = jnp.sum(rs_recv[...], axis=0)
    moment = moments[pl.ds(pl.multiple_of(x * nz, nz), nz), :]
    new_row = DECAY * moment + (1.0 - DECAY) * (row_total / float(total_cols) + TINY)
    ag_recv[x] = new_row
    exchange(ag_recv.at[pl.ds(x, 1)], ag_recv, x, "x", 3)
    wait_all(q_recv, 2)
    row_id = x * (nz * LANES) + iota((nz, LANES), 0) * LANES + iota((nz, LANES), 1)
    valid = row_id < local_rows
    raw_part = jnp.sum(q_recv[...], axis=0) / new_row

    def total_of(value):
        return jnp.sum(jnp.sum(jnp.where(valid, value, 0.0), axis=0, keepdims=True), axis=1, keepdims=True)

    lane = iota((1, LANES), 1)
    row_sum = total_of(new_row) * (1.0 / nz)
    raw_sum = total_of(raw_part)
    pair[core] = jnp.where(
        lane == 0, row_sum, jnp.where(lane == 1, raw_sum, jnp.where(lane == 2, param_local, 0.0))
    )
    pltpu.make_async_remote_copy(
        src_ref=pair.at[core], dst_ref=pair.at[core], send_sem=ssem.at[4], recv_sem=rsem.at[4],
        device_id={"row": 2 * y + 1 - core}, device_id_type=MESH,
    ).start()
    wait_all(pair, 4)
    chip = c * ny + y
    chips[chip] = pair[0] + pair[1]
    for dz, dx in order:
        for dy in range(ny - 1, -1, -1):
            if dz or dx or dy:
                to_row = 2 * lax.rem(y + dy, ny) + core
                to_col = lax.rem(z + dz, nz) * NX + lax.rem(x + dx, NX)
                pltpu.make_async_remote_copy(
                    src_ref=chips.at[chip], dst_ref=chips.at[chip],
                    send_sem=ssem.at[5], recv_sem=rsem.at[5],
                    device_id={"row": to_row, "col": to_col}, device_id_type=MESH,
                ).start()

    wait_all(ag_recv, 3)
    r_o[...] = ag_recv[...].reshape(n_col, LANES)
    col_rsqrt = lax.rsqrt(turned_col)

    def raw_chunk(i):
        size = min(LANES, local_rows - i * LANES)
        factor = lax.rsqrt(ag_recv[i // nz, pl.ds(i % nz, 1), :])
        raw_o[pl.ds(i * LANES, size), :] = (grad[i] * factor * col_rsqrt).T[:size]

    for i in range(pl.cdiv(local_rows, LANES)):
        raw_chunk(i)
    wait_all(chips, 5)
    totals = jnp.sum(chips[...], axis=0)

    def pick_lane(k):
        return jnp.broadcast_to(
            jnp.sum(jnp.where(lane == k, totals, 0.0), axis=1, keepdims=True), (1, LANES)
        )

    mean_row = pick_lane(0) / float(total_rows)
    clip = jnp.maximum(1.0, jnp.sqrt(mean_row * pick_lane(1) / cells))
    root = jnp.sqrt(mean_row)
    step = RATE * jnp.sqrt(pick_lane(2) / cells)
    scal_o[0:1, :] = root / clip
    scal_o[1:2, :] = step
    scal_o[2:3, :] = root
    scal_o[3:8, :] = jnp.zeros((5, LANES), F32)

    sent_all(recv, a2a_ssem)
    for q, buf in enumerate((col_recv, rs_recv, q_recv, ag_recv, pair, chips)):
        sent_all(buf, ssem.at[q])


def write_kernel(
    local_rows, raw, pv, rows, new_col, scal,
    np_o, up_o, nr_o, nc_o, rf_o,
    npv, upv, nrv, ncv, rfv, out_sem, small_sem,
):
    count = 10
    size = local_rows // count
    k = scal[0:1, :]
    step = scal[1:2, :]
    root = scal[2:3, :]
    small = []
    for i in range(count):
        span = pl.ds(i * size, size)
        update = raw[span, :] * k
        upv[span, :] = update
        pltpu.make_async_copy(upv.at[span], up_o.at[span], out_sem.at[0]).start()
        npv[span, :] = pv[span, :] - step * update
        pltpu.make_async_copy(npv.at[span], np_o.at[span], out_sem.at[1]).start()
        if i == 0:
            values = rows[...]
            factor = lax.rsqrt(values) * root
            for j in range(pl.cdiv(local_rows, LANES)):
                n = min(LANES, local_rows - j * LANES)
                nrv[pl.ds(j * LANES, n)] = values[j, :n]
                rfv[pl.ds(j * LANES, n)] = factor[j, :n]
            ncv[...] = new_col[0, :]
            for q, (src, dst) in enumerate(((nrv, nr_o), (rfv, rf_o), (ncv, nc_o))):
                small.append(pltpu.make_async_copy(src, dst, small_sem.at[q]))
                small[-1].start()
    pltpu.make_async_copy(upv, up_o, out_sem.at[0]).wait()
    pltpu.make_async_copy(npv, np_o, out_sem.at[1]).wait()
    for copy in small:
        copy.wait()


def body(n_row, n_col, cotangent, token_ids, param, row_moment, col_moment):
    local_rows, width = param.shape
    total_rows = local_rows * n_row
    total_cols = width * n_col
    nz = n_col // NX
    vmem = pl.BlockSpec(memory_space=pltpu.VMEM)
    hbm = pl.BlockSpec(memory_space=pltpu.HBM)
    dma = pltpu.SemaphoreType.DMA

    ids_shape = (n_col * BLOCK // LANES, LANES)

    def stay(value):
        return pltpu.with_memory_space_constraint(value, pltpu.HBM)

    raw, pv, rows, new_col, scal = pl.pallas_call(
        functools.partial(step_kernel, n_row, n_col, local_rows, total_rows, total_cols),
        out_shape=(
            pltpu.VMEM((local_rows, LANES), F32),
            pltpu.VMEM((local_rows, LANES), F32),
            pltpu.VMEM((n_col, LANES), F32),
            pltpu.VMEM((1, LANES), F32),
            pltpu.VMEM((8, LANES), F32),
        ),
        in_specs=[hbm] * 5,
        out_specs=(vmem,) * 5,
        scratch_shapes=[
            pltpu.VMEM((nz, BLOCK, NX * LANES), BF16),
            pltpu.VMEM(ids_shape, jnp.int32),
            pltpu.VMEM((local_rows,), F32),
            pltpu.VMEM((n_col, LANES), F32),
            pltpu.VMEM((1, LANES), F32),
            pltpu.VMEM(ids_shape, F32),
            pltpu.VMEM(ids_shape, F32),
            pltpu.VMEM(ids_shape, F32),
            pltpu.VMEM((n_col, CAP, LANES), BF16),
            pltpu.VMEM((n_col, CAP, LANES), BF16),
            pltpu.VMEM((2, n_col // 2, GROUP * CAP, 2 * LANES), BF16),
            pltpu.VMEM((nz, NX, CAP, LANES), BF16),
            pltpu.VMEM((n_col, CAP, LANES), BF16),
            pltpu.VMEM((n_col, LANES, LANES), F32),
            pltpu.VMEM((1, 1, LANES), F32),
            pltpu.VMEM((n_row, 1, LANES), F32),
            pltpu.VMEM((NX, nz, LANES), F32),
            pltpu.VMEM((n_col, nz, LANES), F32),
            pltpu.VMEM((NX, nz, LANES), F32),
            pltpu.VMEM((NX, nz, LANES), F32),
            pltpu.VMEM((NX, nz, LANES), F32),
            pltpu.VMEM((2, 1, LANES), F32),
            pltpu.VMEM((n_col * n_row // 2, 1, LANES), F32),
            dma((4,)),
            dma,
            dma,
            dma((n_col // GROUP,)),
            dma((6,)),
            dma((6,)),
        ],
        compiler_params=pltpu.CompilerParams(
            collective_id=0, has_side_effects=True, vmem_limit_bytes=32 * 1024 * 1024
        ),
        name="adafactor_step",
    )(
        stay(cotangent), stay(token_ids.reshape(ids_shape)), stay(param), stay(row_moment),
        stay(col_moment.reshape(1, LANES)),
    )

    return pl.pallas_call(
        functools.partial(write_kernel, local_rows),
        out_shape=(
            jax.ShapeDtypeStruct((local_rows, LANES), F32),
            jax.ShapeDtypeStruct((local_rows, LANES), F32),
            jax.ShapeDtypeStruct((local_rows,), F32),
            jax.ShapeDtypeStruct((LANES,), F32),
            jax.ShapeDtypeStruct((local_rows,), F32),
        ),
        in_specs=[vmem] * 5,
        out_specs=(hbm,) * 5,
        scratch_shapes=[
            pltpu.VMEM((local_rows, LANES), F32),
            pltpu.VMEM((local_rows, LANES), F32),
            pltpu.VMEM((local_rows,), F32),
            pltpu.VMEM((LANES,), F32),
            pltpu.VMEM((local_rows,), F32),
            dma((2,)),
            dma((3,)),
        ],
        compiler_params=pltpu.CompilerParams(vmem_limit_bytes=16 * 1024 * 1024),
        name="adafactor_write",
    )(raw, pv, rows, new_col, scal)


def solution(mesh):
    n_row, n_col = mesh.shape["row"], mesh.shape["col"]
    in_specs = (P("col", None), P(), P("row", "col"), P("row"), P("col"))
    out_specs = (P("row", "col"), P("row", "col"), P("row"), P("col"), P("row"))
    return jax.shard_map(
        functools.partial(body, n_row, n_col),
        mesh=mesh, in_specs=in_specs, out_specs=out_specs, check_vma=False,
    )
```
